256 devices in a mesh: refl: 8 (over x, y_hi), grid: 32 (over z, y_lo, core).
Axes of the slice: x: 4, y: 4 (y_hi: 2, y_lo: 2; y = y_hi * 2 + y_lo), z: 8, core: 2. Of those that a mesh axis runs over, the one named last changes fastest.
Arguments:
- density: bfloat16 [2, 256, 256, 256], P(None, 'grid'), may hold values from -6 to 6
- displacement: bfloat16 [3, 256, 256, 256], P(None, 'grid'), may hold values from -0.8984375 to 0.8984375
- support: int32 [256, 256, 256], P('grid'), may hold values 0 or 1
- millers: int32 [8, 3], replicated, may hold values from -3 to 3
- amplitude: float32 [8, 256, 256, 256], P('refl', None, 'grid'), may hold values from 0.1 to 3
Outputs:
- grad_density: float32 [2, 256, 256, 256], P(None, 'grid', 'refl')
- grad_displacement: float32 [3, 256, 256, 256], P(None, 'grid', 'refl')
The draws below stay inside these ranges and needn't reach their ends.
All inputs are finite; a program needn't handle non-finite values. No bound on the sum of `support` on one device may be relied on, other than what follows from the above.
Results may differ from the reference program's by a relative error of at most 0.00065.
Values sent between devices are 32-bit elements; how exact they have to be, the bound alone decides.
No kernel may reach another device: no remote copies, remote signals or barrier semaphores. Data moves between devices by JAX's collectives and lax.ppermute only.
A program may use at most 128 MiB of HBM per device.

```python
import math
import jax
import jax.numpy as jnp
from jax import lax

N = 256
NREF = 8


def set_ends(values, own_key, low, high):
    place = [jax.random.randint(jax.random.fold_in(own_key, axis), (), 0, length) for axis, length in enumerate(values.shape)]
    widest = values.shape.index(max(values.shape))
    next_to = place[:widest] + [(place[widest] + 1) % values.shape[widest]] + place[widest + 1:]
    return values.at[tuple(place)].set(low).at[tuple(next_to)].set(high)


def levels(stream_key, extent, split, smallest, top_value):
    gain, own = 1.0, jax.random.fold_in(stream_key, 6)
    for dim, shards_of in split:
        heights = jnp.exp(jax.random.uniform(jax.random.fold_in(own, dim), (shards_of,), jnp.float32, smallest / len(split), top_value / len(split)))
        gain = gain * jnp.repeat(heights, extent[dim] // shards_of).reshape([-1 if axis == dim else 1 for axis in range(len(extent))])
    return gain


def gaussian(stream_key, shape, width, bound, pieces=(), dtype=jnp.bfloat16):
    gain = levels(stream_key, shape, pieces, -0.22, 0.18) if pieces else 1.0
    values = jax.random.normal(stream_key, shape, jnp.float32) * width * gain
    return jnp.minimum(jnp.maximum(values, -bound), bound).astype(dtype)


def setup_inputs(seed: int = 0) -> dict:
    streams_of = jax.random.split(jax.random.key(seed), 6)
    density = gaussian(streams_of[0], (2, N, N, N), 1.0, 6.0, ((1, 32),))
    displacement = gaussian(streams_of[1], (3, N, N, N), 0.15, 0.8984375, ((1, 32),))
    support = set_ends((jax.random.randint(streams_of[2], (N, N, N), 0, 4) < 3).astype(jnp.int32), jax.random.fold_in(streams_of[2], 1), 0, 1)
    millers = set_ends(jax.random.randint(streams_of[3], (NREF, 3), -3, 4), jax.random.fold_in(streams_of[3], 1), -3, 3).astype(jnp.int32)
    amplitude = jnp.clip(jnp.exp(math.log(3.0) - 3.4011974 * jax.random.uniform(streams_of[4], (NREF, N, N, N), jnp.float32) ** levels(streams_of[4], (NREF, N, N, N), ((0, 8), (2, 32)), -0.2, 0.2)), 0.1, 3.0)
    return {"density": density, "displacement": displacement, "support": support, "millers": millers, "amplitude": amplitude}


def reference(density, displacement, support, millers, amplitude):
    rho_real = density[0].astype(jnp.float32)
    rho_imag = density[1].astype(jnp.float32)
    shift = displacement.astype(jnp.float32)
    mask = support.astype(jnp.float32)
    indices = millers.astype(jnp.float32)
    grad_real = jnp.zeros_like(rho_real)
    grad_imag = jnp.zeros_like(rho_real)
    grad_shift = jnp.zeros_like(shift)
    for refl_index in range(NREF):
        hkl = indices[refl_index]
        phase = (2.0 * math.pi) * (hkl[0] * shift[0] + hkl[1] * shift[1] + hkl[2] * shift[2])
        cosine = jnp.cos(phase)
        sine = jnp.sin(phase)
        obj_real = mask * (rho_real * cosine - rho_imag * sine)
        obj_imag = mask * (rho_real * sine + rho_imag * cosine)
        spectrum = jnp.fft.fftn(lax.complex(obj_real, obj_imag), norm="ortho")
        magnitude = jnp.abs(spectrum)
        resid = spectrum - (amplitude[refl_index] / jnp.maximum(magnitude, 0.5)) * spectrum
        back = jnp.fft.ifftn(resid, norm="ortho")
        back_real = jnp.real(back)
        back_imag = jnp.imag(back)
        grad_real = grad_real + mask * (cosine * back_real + sine * back_imag)
        grad_imag = grad_imag + mask * (cosine * back_imag - sine * back_real)
        twist = obj_real * back_imag - obj_imag * back_real
        grad_shift = grad_shift + hkl[:, None, None, None] * twist[None]
    scale = 1.0 / NREF
    return jnp.stack([grad_real, grad_imag]) * scale, grad_shift * scale
```

```python
import functools
import math

import jax
import jax.numpy as jnp
import ml_dtypes
import numpy as np
from jax import lax
from jax.experimental import pallas as pl
from jax.experimental.pallas import tpu as pltpu
from jax.sharding import PartitionSpec as P

N = 256
CH = 2
KC = N // CH
SLABS = 32
XL = 8
NREF = 8
BF = jnp.bfloat16
F32 = jnp.float32


def split_np(table):
    high = table.astype(ml_dtypes.bfloat16)
    low = (table - high.astype(np.float64)).astype(ml_dtypes.bfloat16)
    return high, low


def dft_np():
    n = np.arange(N)
    angle = 2.0 * np.pi * (np.outer(n, n) % N) / N
    return np.cos(angle) / math.sqrt(N), -np.sin(angle) / math.sqrt(N)


def left_table(inverse):
    re, im = dft_np()
    high, low = split_np(np.concatenate([re, -im if inverse else im], 0))
    return np.concatenate([high, high, low], 1)


def packed_columns():
    chunk = np.arange(N) // KC
    inner = np.arange(N) % KC
    real = chunk * 2 * KC + inner
    return real, real + KC


def right_forward():
    re, im = dft_np()
    real, imag = packed_columns()
    table = np.zeros((2 * N, 2 * N))
    table[:N, real] = re
    table[:N, imag] = im
    table[N:, real] = -im
    table[N:, imag] = re
    high, low = split_np(table)
    return np.concatenate([high, high, low], 0)


def right_inverse():
    re, im = dft_np()
    real, imag = packed_columns()
    table = np.zeros((2 * N, 2 * N))
    table[real, :N] = re
    table[real, N:] = -im
    table[imag, :N] = im
    table[imag, N:] = re
    return split_np(table)


def sine_coefficients():
    b = 0.25 * np.cos((np.arange(400) + 0.5) / 400 * np.pi / 2)
    powers = np.stack([b ** (2 * k + 1) for k in range(6)], 1)
    return [float(v) for v in np.linalg.lstsq(powers, np.sin(2 * np.pi * b), rcond=None)[0]]


SINE = sine_coefficients()


def sine_turns(b):
    q = b * b
    acc = jnp.full_like(b, SINE[5])
    for k in range(4, -1, -1):
        acc = acc * q + SINE[k]
    return acc * b


def cos_sin_turns(t):
    t = t - jnp.round(t)
    cosine = sine_turns(0.25 - jnp.abs(t))
    u = t - 0.25
    u = u - jnp.round(u)
    return cosine, sine_turns(0.25 - jnp.abs(u))


def split(value):
    high = value.astype(BF)
    return high, (value - high.astype(F32)).astype(BF)


def left_multiply(table, packed):
    high, low = split(packed)
    both = jnp.dot(table, jnp.concatenate([high, low, high], 0), preferred_element_type=F32)
    real = both[:N, :KC] - both[N:, KC:]
    imag = both[:N, KC:] + both[N:, :KC]
    return jnp.concatenate([real, imag], 1)


def object_kernel(idx_ref, miller_ref, rho_ref, shift_ref, support_ref, table_ref, out_ref, high_ref, low_ref):
    r = idx_ref[0]
    h = miller_ref[r, 0].astype(F32)
    k = miller_ref[r, 1].astype(F32)
    l = miller_ref[r, 2].astype(F32)
    rows = 32

    def step(i, carry):
        at = pl.ds(pl.multiple_of(i * rows, rows), rows)
        u = [shift_ref[c, 0, at, :].astype(F32) for c in range(3)]
        mask = support_ref[0, at, :].astype(F32)
        cosine, sine = cos_sin_turns(h * u[0] + k * u[1] + l * u[2])
        real = mask * rho_ref[0, 0, at, :].astype(F32)
        imag = mask * rho_ref[1, 0, at, :].astype(F32)
        for part, value in enumerate((real * cosine - imag * sine, real * sine + imag * cosine)):
            high, low = split(value)
            high_ref[at, part * N : (part + 1) * N] = high
            low_ref[at, part * N : (part + 1) * N] = low
        return carry

    lax.fori_loop(0, N // rows, step, 0)
    high = high_ref[...]
    out_ref[0] = jnp.dot(
        jnp.concatenate([high, low_ref[...], high], 1), table_ref[...], preferred_element_type=F32
    )


def y_forward_kernel(a_ref, table_ref, out_ref):
    def step(x, carry):
        out_ref[:, x] = left_multiply(table_ref[...], a_ref[x]).reshape(SLABS, XL, 2 * KC)
        return carry

    lax.fori_loop(0, XL, step, 0)


def x_kernel(in_ref, amp_ref, forward_ref, inverse_ref, out_ref, real_ref, imag_ref):
    real_ref[...] = in_ref[:, :KC]
    imag_ref[...] = in_ref[:, KC:]

    def step(i, carry):
        at = pl.ds(i, N, stride=XL)
        spec = left_multiply(forward_ref[...], jnp.concatenate([real_ref[at, :], imag_ref[at, :]], 1))
        real, imag = spec[:, :KC], spec[:, KC:]
        ratio = amp_ref[at, :] * lax.rsqrt(jnp.maximum(real * real + imag * imag, 0.25))
        resid = jnp.concatenate([real - ratio * real, imag - ratio * imag], 1)
        back = left_multiply(inverse_ref[...], resid)
        real_ref[at, :] = back[:, :KC]
        imag_ref[at, :] = back[:, KC:]
        return carry

    lax.fori_loop(0, XL, step, 0)
    out_ref[:, :KC] = real_ref[...]
    out_ref[:, KC:] = imag_ref[...]


def y_inverse_kernel(idx_ref, in_ref, table_ref, *refs):
    outs, t_ref = refs[:NREF], refs[NREF]
    r = idx_ref[0]

    def step(x, carry):
        t_ref[...] = left_multiply(table_ref[...], in_ref[:, x].reshape(N, 2 * KC))
        for s in range(NREF):
            start = pl.multiple_of(lax.rem(r + s, NREF) * 32, 32)
            outs[s][x] = t_ref[pl.ds(start, 32), :]
        return carry

    lax.fori_loop(0, XL, step, 0)


def gradient_kernel(shift_by, idx_ref, miller_ref, rho_ref, shift_ref, support_ref, *refs):
    ins, high_ref, low_ref = refs[:CH], refs[CH], refs[CH + 1]
    sums = refs[CH + 2 : -3]
    rho_out, shift_out, back_ref = refs[-3:]
    g = lax.rem(idx_ref[0] + NREF - shift_by, NREF)
    h = miller_ref[g, 0].astype(F32)
    k = miller_ref[g, 1].astype(F32)
    l = miller_ref[g, 2].astype(F32)
    high, low = split(jnp.concatenate([ref[...].reshape(N, 2 * KC) for ref in ins], 1))
    dot = functools.partial(jnp.dot, preferred_element_type=F32)
    back_ref[...] = dot(high, high_ref[...]) + dot(low, high_ref[...]) + dot(high, low_ref[...])

    def step(x, carry):
        at = pl.ds(pl.multiple_of(x * 32, 32), 32)
        u = [shift_ref[c, x].astype(F32) for c in range(3)]
        mask = support_ref[x].astype(F32) * (1.0 / NREF)
        cosine, sine = cos_sin_turns(h * u[0] + k * u[1] + l * u[2])
        real, imag = back_ref[at, :N], back_ref[at, N:]
        p = mask * (cosine * real + sine * imag)
        q = mask * (cosine * imag - sine * real)
        twist = rho_ref[0, x].astype(F32) * q - rho_ref[1, x].astype(F32) * p
        for out, old, n, value in (
            (rho_out, 0, 0, p),
            (rho_out, 0, 1, q),
            (shift_out, 1, 0, h * twist),
            (shift_out, 1, 1, k * twist),
            (shift_out, 1, 2, l * twist),
        ):
            out[n, x] = sums[old][n, x] + value if sums else value
        return carry

    lax.fori_loop(0, XL, step, 0)


SMEM = pl.BlockSpec(memory_space=pltpu.SMEM)
VMEM = pl.BlockSpec(memory_space=pltpu.VMEM)


def cost(flops, size):
    return pl.CostEstimate(flops=int(flops), bytes_accessed=int(size), transcendentals=0)


def f32(*shape):
    return jax.ShapeDtypeStruct(shape, F32)


def params(mib):
    return pltpu.CompilerParams(vmem_limit_bytes=mib * 1024 * 1024)


def after(value, *earlier):
    return lax.optimization_barrier((value, earlier))[0]


def body(density, displacement, support, millers, amplitude):
    r = lax.axis_index("refl")
    idx = jnp.stack([r]).astype(jnp.int32)
    forward, inverse = jnp.asarray(left_table(False)), jnp.asarray(left_table(True))
    high, low = (jnp.asarray(t) for t in right_inverse())
    amp = amplitude.reshape(N * XL, N)
    a = pl.pallas_call(
        object_kernel,
        grid=(XL,),
        in_specs=[
            SMEM,
            SMEM,
            pl.BlockSpec((2, 1, N, N), lambda x: (0, x, 0, 0)),
            pl.BlockSpec((3, 1, N, N), lambda x: (0, x, 0, 0)),
            pl.BlockSpec((1, N, N), lambda x: (x, 0, 0)),
            pl.BlockSpec((6 * N, 2 * N), lambda x: (0, 0)),
        ],
        out_specs=pl.BlockSpec((1, N, 2 * N), lambda x: (x, 0, 0)),
        out_shape=f32(XL, N, 2 * N),
        scratch_shapes=[pltpu.VMEM((N, 2 * N), BF)] * 2,
        compiler_params=params(24),
        cost_estimate=cost(3.2e9, 12e6),
        name="object_z",
    )(idx, millers, density, displacement, support, jnp.asarray(right_forward()))

    def y_forward(c):
        return pl.pallas_call(
            y_forward_kernel,
            grid=(1,),
            in_specs=[pl.BlockSpec((XL, N, 2 * KC), lambda i: (0, 0, c)), VMEM],
            out_specs=VMEM,
            out_shape=f32(SLABS, XL, XL, 2 * KC),
            compiler_params=params(24),
            cost_estimate=cost(3.2e9, 12e6),
            name=f"y_forward_{c}",
        )(a, forward)

    def x_both(c, part):
        return pl.pallas_call(
            x_kernel,
            grid=(1,),
            in_specs=[VMEM, pl.BlockSpec((N * XL, KC), lambda i: (0, c)), VMEM, VMEM],
            out_specs=VMEM,
            out_shape=f32(N * XL, 2 * KC),
            scratch_shapes=[pltpu.VMEM((N * XL, KC), F32)] * 2,
            compiler_params=params(24),
            cost_estimate=cost(6.4e9, 24e6),
            name=f"x_{c}",
        )(part.reshape(N * XL, 2 * KC), amp, forward, inverse).reshape(SLABS, XL, XL, 2 * KC)

    def y_inverse(c, part):
        return pl.pallas_call(
            y_inverse_kernel,
            in_specs=[SMEM, VMEM, VMEM],
            out_specs=[VMEM] * NREF,
            out_shape=[f32(XL, 32, 2 * KC)] * NREF,
            scratch_shapes=[pltpu.VMEM((N, 2 * KC), F32)],
            compiler_params=params(24),
            cost_estimate=cost(3.2e9, 12e6),
            name=f"y_inverse_{c}",
        )(idx, part, inverse)

    def over_grid(part):
        return lax.all_to_all(part, "grid", 0, 0, tiled=True)

    def over_refl(parts):
        ring = lambda s: [(i, (i + s) % NREF) for i in range(NREF)]
        moved = {s: lax.ppermute(parts[s], "refl", ring(s)) for s in R_ORDER}
        return [parts[0]] + [moved[s] for s in range(1, NREF)]

    def gradient(s, parts, sums):
        out_block = lambda n: pl.BlockSpec((n, XL, 32, N), lambda i, idx: (0, 0, 0, 0))
        whole = lambda i, idx: (0, 0)
        return pl.pallas_call(
            functools.partial(gradient_kernel, s),
            grid_spec=pltpu.PrefetchScalarGridSpec(
                num_scalar_prefetch=1,
                grid=(1,),
                in_specs=[
                    SMEM,
                    pl.BlockSpec((2, XL, 32, N), lambda i, idx: (0, 0, idx[0], 0)),
                    pl.BlockSpec((3, XL, 32, N), lambda i, idx: (0, 0, idx[0], 0)),
                    pl.BlockSpec((XL, 32, N), lambda i, idx: (0, idx[0], 0)),
                ]
                + [pl.BlockSpec((XL, 32, 2 * KC), lambda i, idx: (0, 0, 0))] * CH
                + [pl.BlockSpec((2 * N, 2 * N), whole)] * 2
                + ([out_block(2), out_block(3)] if sums else []),
                out_specs=[out_block(2), out_block(3)],
                scratch_shapes=[pltpu.VMEM((N, 2 * N), F32)],
            ),
            out_shape=[f32(2, XL, 32, N), f32(3, XL, 32, N)],
            compiler_params=params(24),
            cost_estimate=cost(0.8e9, 5e6),
            name=f"gradient_{s}",
        )(idx, millers, density, displacement, support, *parts, high, low, *sums)

    f0 = over_grid(y_forward(0))
    f1 = over_grid(after(y_forward(1), f0))
    b0 = over_grid(after(x_both(0, f0), f1))
    b1 = over_grid(after(x_both(1, f1), b0))
    r0 = over_refl(y_inverse(0, b0))
    r1 = over_refl(y_inverse(1, after(b1, *r0)))
    sums = ()
    for s in (0,) + R_ORDER:
        sums = tuple(gradient(s, (r0[s], r1[s]), sums))
    return sums


R_ORDER = (4, 3, 5, 2, 6, 1, 7)


def solution(mesh):
    in_specs = (
        P(None, "grid", None, None),
        P(None, "grid", None, None),
        P("grid", None, None),
        P(),
        P("refl", None, "grid", None),
    )
    out_specs = (P(None, "grid", "refl", None), P(None, "grid", "refl", None))
    return jax.shard_map(body, mesh=mesh, in_specs=in_specs, out_specs=out_specs, check_vma=False)
```

```python
import functools
import math

import jax
import jax.numpy as jnp
import ml_dtypes
import numpy as np
from jax import lax
from jax.experimental import pallas as pl
from jax.experimental.pallas import tpu as pltpu
from jax.sharding import PartitionSpec as P

N = 256
CH = 2
KC = N // CH
SLABS = 32
XL = 8
NREF = 8
HEAD_ROWS = 32
HALF = XL // 2
R_ORDER = (4, 3, 5, 2, 6, 1, 7)
BF = jnp.bfloat16
F32 = jnp.float32


def split_np(table):
    high = table.astype(ml_dtypes.bfloat16)
    low = (table - high.astype(np.float64)).astype(ml_dtypes.bfloat16)
    return high, low


def dft_np():
    n = np.arange(N)
    angle = 2.0 * np.pi * (np.outer(n, n) % N) / N
    return np.cos(angle) / math.sqrt(N), -np.sin(angle) / math.sqrt(N)


def left_table(inverse):
    re, im = dft_np()
    high, low = split_np(np.concatenate([re, -im if inverse else im], 0))
    return np.concatenate([high, high, low], 1)


def halves_of_slabs(table):
    rows = np.arange(N).reshape(SLABS, 2, XL // 2).transpose(1, 0, 2).reshape(-1)
    return table[np.concatenate([rows, rows + N])]


def packed_columns():
    chunk = np.arange(N) // KC
    inner = np.arange(N) % KC
    real = chunk * 2 * KC + inner
    return real, real + KC


def right_forward():
    re, im = dft_np()
    real, imag = packed_columns()
    table = np.zeros((2 * N, 2 * N))
    table[:N, real] = re
    table[:N, imag] = im
    table[N:, real] = -im
    table[N:, imag] = re
    high, low = split_np(table)
    return np.concatenate([high, high, low], 0)


def right_inverse():
    re, im = dft_np()
    real, imag = packed_columns()
    table = np.zeros((2 * N, 2 * N))
    table[real, :N] = re
    table[real, N:] = -im
    table[imag, :N] = im
    table[imag, N:] = re
    return split_np(table)


def sine_coefficients():
    b = 0.25 * np.cos((np.arange(400) + 0.5) / 400 * np.pi / 2)
    powers = np.stack([b ** (2 * k + 1) for k in range(6)], 1)
    return [float(v) for v in np.linalg.lstsq(powers, np.sin(2 * np.pi * b), rcond=None)[0]]


SINE = sine_coefficients()


def sine_turns(b):
    q = b * b
    acc = jnp.full_like(b, SINE[5])
    for k in range(4, -1, -1):
        acc = acc * q + SINE[k]
    return acc * b


def cos_sin_turns(t):
    t = t - jnp.round(t)
    cosine = sine_turns(0.25 - jnp.abs(t))
    u = t - 0.25
    u = u - jnp.round(u)
    return cosine, sine_turns(0.25 - jnp.abs(u))


def split(value):
    high = value.astype(BF)
    return high, (value - high.astype(F32)).astype(BF)


def left_multiply(table, packed):
    return left_split(table, *split(packed))


def left_split(table, high, low):
    both = jnp.dot(table, jnp.concatenate([high, low, high], 0), preferred_element_type=F32)
    real = both[:N, :KC] - both[N:, KC:]
    imag = both[:N, KC:] + both[N:, :KC]
    return jnp.concatenate([real, imag], 1)


def object_rows(hkl, rho_ref, shift_ref, support_ref, high_ref, low_ref, start, rows):
    at = pl.ds(start, rows)
    u = [shift_ref[c, 0, at, :].astype(F32) for c in range(3)]
    mask = support_ref[0, at, :].astype(F32)
    cosine, sine = cos_sin_turns(hkl[0] * u[0] + hkl[1] * u[1] + hkl[2] * u[2])
    real = mask * rho_ref[0, 0, at, :].astype(F32)
    imag = mask * rho_ref[1, 0, at, :].astype(F32)
    for part, value in enumerate((real * cosine - imag * sine, real * sine + imag * cosine)):
        high, low = split(value)
        high_ref[at, part * N : (part + 1) * N] = high
        low_ref[at, part * N : (part + 1) * N] = low


def head_kernel(miller_ref, rho_ref, shift_ref, support_ref, table_ref, left_ref, out_ref, high_ref, low_ref, ah_ref, al_ref):
    i = pl.program_id(0)
    r = lax.axis_index("refl")
    hkl = [miller_ref[c, r].astype(F32) for c in range(3)]
    now, before = lax.rem(i, 2), lax.rem(i + 1, 2)
    out_ref[:, 0] = left_split(left_ref[...], ah_ref[now], al_ref[now]).reshape(SLABS, XL, 2 * KC)
    high = high_ref[before]
    a = jnp.dot(jnp.concatenate([high, low_ref[before], high], 1), table_ref[...], preferred_element_type=F32)
    ah_ref[before], al_ref[before] = split(a)
    for row in range(0, N, HEAD_ROWS):
        object_rows(hkl, rho_ref, shift_ref, support_ref, high_ref.at[now], low_ref.at[now], row, HEAD_ROWS)


def x_kernel(in_ref, amp_ref, forward_ref, inverse_ref, *refs):
    outs, (real_ref, imag_ref, sems) = refs[:-3], refs[-3:]
    parts = ((real_ref, pl.ds(0, KC)), (imag_ref, pl.ds(KC, KC)))
    copies = [
        pltpu.make_async_copy(in_ref.at[:, lanes], part, sems.at[i]) for i, (part, lanes) in enumerate(parts)
    ]
    for copy in copies:
        copy.start()
    for copy in copies:
        copy.wait()

    def step(i, carry):
        at = pl.ds(i, N, stride=XL)
        spec = left_multiply(forward_ref[...], jnp.concatenate([real_ref[at, :], imag_ref[at, :]], 1))
        real, imag = spec[:, :KC], spec[:, KC:]
        ratio = amp_ref[at, :] * lax.rsqrt(jnp.maximum(real * real + imag * imag, 0.25))
        resid = jnp.concatenate([real - ratio * real, imag - ratio * imag], 1)
        back = left_multiply(inverse_ref[...], resid)
        real_ref[at, :] = back[:, :KC]
        imag_ref[at, :] = back[:, KC:]
        return carry

    lax.fori_loop(0, XL, step, 0)
    rows = N * XL // len(outs)
    copies = [
        pltpu.make_async_copy(part.at[pl.ds(n * rows, rows), :], out.at[:, lanes], sems.at[2 * n + i])
        for n, out in enumerate(outs)
        for i, (part, lanes) in enumerate(parts)
    ]
    for copy in copies:
        copy.start()
    for copy in copies:
        copy.wait()


def y_inverse_kernel(idx_ref, in_ref, table_ref, *refs):
    outs, (u_ref, t_ref, sems) = refs[:NREF], refs[NREF:]
    r = idx_ref[0]
    planes = u_ref.shape[0]
    copies = [pltpu.make_async_copy(in_ref.at[:, x], u_ref.at[x], sems.at[x]) for x in range(planes)]
    for copy in copies:
        copy.start()
    for x in range(planes):
        copies[x].wait()
        t_ref[x] = left_multiply(table_ref[...], u_ref[x].reshape(N, 2 * KC))
    copies = []
    for s in range(NREF):
        start = pl.multiple_of(lax.rem(r + s, NREF) * 32, 32)
        if planes < XL:
            outs[s][...] = t_ref[:, pl.ds(start, 32), :]
        else:
            copies.append(pltpu.make_async_copy(t_ref.at[:, pl.ds(start, 32), :], outs[s], sems.at[s]))
            copies[-1].start()
    for copy in copies:
        copy.wait()


def gradient_kernel(shift_by, adds, idx_ref, miller_ref, rho_ref, shift_ref, support_ref, *refs):
    ins, high_ref, low_ref = refs[:CH], refs[CH], refs[CH + 1]
    sums = refs[CH + 2 : -3]
    rho_out, shift_out, back_ref = refs[-3:]
    g = lax.rem(idx_ref[0] + NREF - shift_by, NREF)
    h, k, l = (miller_ref[c, g].astype(F32) for c in range(3))
    high, low = split(jnp.concatenate([ref[...].reshape(HALF * 32, 2 * KC) for ref in ins], 1))
    dot = functools.partial(jnp.dot, preferred_element_type=F32)
    back_ref[...] = dot(high, high_ref[...]) + dot(low, high_ref[...]) + dot(high, low_ref[...])

    def step(x, carry):
        at = pl.ds(pl.multiple_of(x * 32, 32), 32)
        u = [shift_ref[c, x].astype(F32) for c in range(3)]
        mask = support_ref[x].astype(F32) * (1.0 / NREF)
        cosine, sine = cos_sin_turns(h * u[0] + k * u[1] + l * u[2])
        real, imag = back_ref[at, :N], back_ref[at, N:]
        p = mask * (cosine * real + sine * imag)
        q = mask * (cosine * imag - sine * real)
        twist = rho_ref[0, x].astype(F32) * q - rho_ref[1, x].astype(F32) * p
        for out, old, n, value in (
            (rho_out, 0, 0, p),
            (rho_out, 0, 1, q),
            (shift_out, 1, 0, h * twist),
            (shift_out, 1, 1, k * twist),
            (shift_out, 1, 2, l * twist),
        ):
            out[n, x] = sums[old][n, x] + value if adds else value
        return carry

    lax.fori_loop(0, HALF, step, 0)


SMEM = pl.BlockSpec(memory_space=pltpu.SMEM)
VMEM = pl.BlockSpec(memory_space=pltpu.VMEM)
HBM = pl.BlockSpec(memory_space=pltpu.HBM)


def cost(flops, size):
    return pl.CostEstimate(flops=int(flops), bytes_accessed=int(size), transcendentals=0)


def f32(*shape):
    return jax.ShapeDtypeStruct(shape, F32)


def params(mib):
    return pltpu.CompilerParams(vmem_limit_bytes=mib * 1024 * 1024)


def hbm(*shape):
    return pltpu.HBM(shape, F32)


def in_hbm(value):
    return pltpu.with_memory_space_constraint(value, pltpu.HBM)


def after(value, *earlier):
    return lax.optimization_barrier((value, earlier))[0]


def head(c, millers, density, displacement, support):
    plane = lambda i: jnp.minimum(i, XL - 1)
    last = lambda i: jnp.maximum(i - 2, 0)
    return pl.pallas_call(
        head_kernel,
        grid=(XL + 2,),
        in_specs=[
            SMEM,
            pl.BlockSpec((2, 1, N, N), lambda i: (0, plane(i), 0, 0)),
            pl.BlockSpec((3, 1, N, N), lambda i: (0, plane(i), 0, 0)),
            pl.BlockSpec((1, N, N), lambda i: (plane(i), 0, 0)),
            pl.BlockSpec((6 * N, 2 * KC), lambda i: (0, c)),
            pl.BlockSpec((2 * N, 3 * N), lambda i: (0, 0)),
        ],
        out_specs=pl.BlockSpec((SLABS, 1, XL, 2 * KC), lambda i: (0, last(i), 0, 0)),
        out_shape=f32(SLABS, XL, XL, 2 * KC),
        scratch_shapes=[pltpu.VMEM((2, N, 2 * N), BF)] * 2 + [pltpu.VMEM((2, N, 2 * KC), BF)] * 2,
        compiler_params=params(60),
        cost_estimate=cost(6.4e9, 16e6),
        name=f"head_{c}",
    )(millers, density, displacement, support, jnp.asarray(right_forward()), jnp.asarray(left_table(False)))


def body(density, displacement, support, millers, amplitude):
    r = lax.axis_index("refl")
    idx = jnp.stack([r]).astype(jnp.int32)
    forward, inverse = jnp.asarray(left_table(False)), jnp.asarray(left_table(True))
    high, low = (jnp.asarray(t) for t in right_inverse())
    amp = amplitude.reshape(N * XL, N)
    millers = millers.T

    def x_both(c, part):
        pieces = c + 1
        table = inverse if c == 0 else jnp.asarray(halves_of_slabs(left_table(True)))
        parts = pl.pallas_call(
            x_kernel,
            grid=(1,),
            in_specs=[HBM, pl.BlockSpec((N * XL, KC), lambda i: (0, c)), VMEM, VMEM],
            out_specs=[HBM] * pieces,
            out_shape=[hbm(N * XL // pieces, 2 * KC)] * pieces,
            scratch_shapes=[pltpu.VMEM((N * XL, KC), F32)] * 2 + [pltpu.SemaphoreType.DMA((4,))],
            compiler_params=params(24),
            cost_estimate=cost(6.4e9, 24e6),
            name=f"x_{c}",
        )(in_hbm(part.reshape(N * XL, 2 * KC)), amp, forward, table)
        return [p.reshape(SLABS, XL // pieces, XL, 2 * KC) for p in parts]

    def y_inverse(name, part):
        planes = part.shape[1]
        return pl.pallas_call(
            y_inverse_kernel,
            in_specs=[SMEM, HBM, VMEM],
            out_specs=[VMEM if planes < XL else HBM] * NREF,
            out_shape=[(f32 if planes < XL else hbm)(planes, 32, 2 * KC)] * NREF,
            scratch_shapes=[
                pltpu.VMEM((planes, SLABS, XL, 2 * KC), F32),
                pltpu.VMEM((planes, N, 2 * KC), F32),
                pltpu.SemaphoreType.DMA((XL,)),
            ],
            compiler_params=params(24),
            cost_estimate=cost(0.4e9 * planes, 1.5e6 * planes),
            name=f"y_inverse_{name}",
        )(idx, in_hbm(part), inverse)

    def over_grid(part):
        return lax.all_to_all(part, "grid", 0, 0, tiled=True)

    def over_refl(parts):
        ring = lambda s: [(i, (i + s) % NREF) for i in range(NREF)]
        moved = {s: lax.ppermute(parts[s], "refl", ring(s)) for s in R_ORDER}
        return [parts[0]] + [moved[s] for s in range(1, NREF)]

    def gradient(s, half, parts, sums):
        adds = s > 0
        out_block = lambda n: pl.BlockSpec((n, HALF, 32, N), lambda i, idx: (0, half, 0, 0))
        whole = lambda i, idx: (0, 0)
        return tuple(
            pl.pallas_call(
                functools.partial(gradient_kernel, s, adds),
                grid_spec=pltpu.PrefetchScalarGridSpec(
                    num_scalar_prefetch=1,
                    grid=(1,),
                    in_specs=[
                        SMEM,
                        pl.BlockSpec((2, HALF, 32, N), lambda i, idx: (0, half, idx[0], 0)),
                        pl.BlockSpec((3, HALF, 32, N), lambda i, idx: (0, half, idx[0], 0)),
                        pl.BlockSpec((HALF, 32, N), lambda i, idx: (half, idx[0], 0)),
                        pl.BlockSpec((HALF, 32, 2 * KC), lambda i, idx: (half, 0, 0)),
                        pl.BlockSpec((HALF, 32, 2 * KC), lambda i, idx: (0, 0, 0)),
                    ]
                    + [pl.BlockSpec((2 * N, 2 * N), whole)] * 2
                    + [out_block(2 + n) if adds else pl.BlockSpec(memory_space=pl.ANY) for n, _ in enumerate(sums)],
                    out_specs=[out_block(2), out_block(3)],
                    scratch_shapes=[pltpu.VMEM((HALF * 32, 2 * N), F32)],
                ),
                out_shape=[f32(2, XL, 32, N), f32(3, XL, 32, N)],
                input_output_aliases={9 + n: n for n, _ in enumerate(sums)},
                compiler_params=params(24),
                cost_estimate=cost(0.4e9, 3e6),
                name=f"gradient_{half}_{s}",
            )(idx, millers, density, displacement, support, *parts, high, low, *sums)
        )

    f0 = over_grid(head(0, millers, density, displacement, support))
    f1 = over_grid(after(head(1, millers, density, displacement, support), f0))
    b0 = over_grid(after(x_both(0, f0)[0], f1))
    halves = x_both(1, f1)
    b1 = [over_grid(after(halves[0], b0))]
    r0 = over_refl(y_inverse("0", b0))
    b1.append(over_grid(after(halves[1], b1[0], *(r0[s] for s in R_ORDER[:4]))))
    r1 = over_refl(y_inverse("1a", after(b1[0], *r0)))
    sums = ()
    for s in (0,) + R_ORDER:
        sums = gradient(s, 0, (in_hbm(r0[s]), r1[s]), sums)
    r1 = over_refl(y_inverse("1b", after(b1[1], *sums)))
    for s in (0,) + R_ORDER:
        sums = gradient(s, 1, (in_hbm(r0[s]), r1[s]), sums)
    return sums


def solution(mesh):
    in_specs = (
        P(None, "grid", None, None),
        P(None, "grid", None, None),
        P("grid", None, None),
        P(),
        P("refl", None, "grid", None),
    )
    out_specs = (P(None, "grid", "refl", None), P(None, "grid", "refl", None))
    return jax.shard_map(body, mesh=mesh, in_specs=in_specs, out_specs=out_specs, check_vma=False)
```

```python
import functools
import math

import jax
import jax.numpy as jnp
import ml_dtypes
import numpy as np
from jax import lax
from jax.experimental import pallas as pl
from jax.experimental.pallas import tpu as pltpu
from jax.sharding import PartitionSpec as P

N = 256
CH = 2
KC = N // CH
SLABS = 32
XL = 8
NREF = 8
HEAD_ROWS = 32
R_ORDER = (4, 3, 5, 2, 6, 1, 7)
BF = jnp.bfloat16
F32 = jnp.float32


def split_np(table):
    high = table.astype(ml_dtypes.bfloat16)
    low = (table - high.astype(np.float64)).astype(ml_dtypes.bfloat16)
    return high, low


def dft_np():
    n = np.arange(N)
    angle = 2.0 * np.pi * (np.outer(n, n) % N) / N
    return np.cos(angle) / math.sqrt(N), -np.sin(angle) / math.sqrt(N)


def left_table(inverse):
    re, im = dft_np()
    high, low = split_np(np.concatenate([re, -im if inverse else im], 0))
    return np.concatenate([high, high, low], 1)


def packed_columns():
    chunk = np.arange(N) // KC
    inner = np.arange(N) % KC
    real = chunk * 2 * KC + inner
    return real, real + KC


def right_forward():
    re, im = dft_np()
    real, imag = packed_columns()
    table = np.zeros((2 * N, 2 * N))
    table[:N, real] = re
    table[:N, imag] = im
    table[N:, real] = -im
    table[N:, imag] = re
    high, low = split_np(table)
    return np.concatenate([high, high, low], 0)


def right_inverse():
    re, im = dft_np()
    real, imag = packed_columns()
    table = np.zeros((2 * N, 2 * N))
    table[real, :N] = re
    table[real, N:] = -im
    table[imag, :N] = im
    table[imag, N:] = re
    return split_np(table)


def sine_coefficients():
    b = 0.25 * np.cos((np.arange(400) + 0.5) / 400 * np.pi / 2)
    powers = np.stack([b ** (2 * k + 1) for k in range(6)], 1)
    return [float(v) for v in np.linalg.lstsq(powers, np.sin(2 * np.pi * b), rcond=None)[0]]


SINE = sine_coefficients()


def sine_turns(b):
    q = b * b
    acc = jnp.full_like(b, SINE[5])
    for k in range(4, -1, -1):
        acc = acc * q + SINE[k]
    return acc * b


def cos_sin_turns(t):
    t = t - jnp.round(t)
    cosine = sine_turns(0.25 - jnp.abs(t))
    u = t - 0.25
    u = u - jnp.round(u)
    return cosine, sine_turns(0.25 - jnp.abs(u))


def split(value):
    high = value.astype(BF)
    return high, (value - high.astype(F32)).astype(BF)


def left_multiply(table, packed):
    return left_split(table, *split(packed))


def left_split(table, high, low):
    both = jnp.dot(table, jnp.concatenate([high, low, high], 0), preferred_element_type=F32)
    real = both[:N, :KC] - both[N:, KC:]
    imag = both[:N, KC:] + both[N:, :KC]
    return jnp.concatenate([real, imag], 1)


def object_rows(hkl, rho_ref, shift_ref, support_ref, high_ref, low_ref, start, rows):
    at = pl.ds(start, rows)
    u = [shift_ref[c, 0, at, :].astype(F32) for c in range(3)]
    mask = support_ref[0, at, :].astype(F32)
    cosine, sine = cos_sin_turns(hkl[0] * u[0] + hkl[1] * u[1] + hkl[2] * u[2])
    real = mask * rho_ref[0, 0, at, :].astype(F32)
    imag = mask * rho_ref[1, 0, at, :].astype(F32)
    for part, value in enumerate((real * cosine - imag * sine, real * sine + imag * cosine)):
        high, low = split(value)
        high_ref[at, part * N : (part + 1) * N] = high
        low_ref[at, part * N : (part + 1) * N] = low


def head_kernel(miller_ref, rho_ref, shift_ref, support_ref, table_ref, left_ref, out_ref, high_ref, low_ref, ah_ref, al_ref):
    i = pl.program_id(0)
    r = lax.axis_index("refl")
    hkl = [miller_ref[c, r].astype(F32) for c in range(3)]
    now, before = lax.rem(i, 2), lax.rem(i + 1, 2)
    out_ref[:, 0] = left_split(left_ref[...], ah_ref[now], al_ref[now]).reshape(SLABS, XL, 2 * KC)
    high = high_ref[before]
    a = jnp.dot(jnp.concatenate([high, low_ref[before], high], 1), table_ref[...], preferred_element_type=F32)
    ah_ref[before], al_ref[before] = split(a)
    for row in range(0, N, HEAD_ROWS):
        object_rows(hkl, rho_ref, shift_ref, support_ref, high_ref.at[now], low_ref.at[now], row, HEAD_ROWS)


def x_kernel(in_ref, amp_ref, forward_ref, inverse_ref, *refs):
    out_ref, real_ref, imag_ref, sems = refs
    parts = ((real_ref, pl.ds(0, KC)), (imag_ref, pl.ds(KC, KC)))
    copies = [
        pltpu.make_async_copy(in_ref.at[:, lanes], part, sems.at[i]) for i, (part, lanes) in enumerate(parts)
    ]
    for copy in copies:
        copy.start()
    for copy in copies:
        copy.wait()

    def step(i, carry):
        at = pl.ds(i, N, stride=XL)
        spec = left_multiply(forward_ref[...], jnp.concatenate([real_ref[at, :], imag_ref[at, :]], 1))
        real, imag = spec[:, :KC], spec[:, KC:]
        ratio = amp_ref[at, :] * lax.rsqrt(jnp.maximum(real * real + imag * imag, 0.25))
        resid = jnp.concatenate([real - ratio * real, imag - ratio * imag], 1)
        back = left_multiply(inverse_ref[...], resid)
        real_ref[at, :] = back[:, :KC]
        imag_ref[at, :] = back[:, KC:]
        return carry

    lax.fori_loop(0, XL, step, 0)
    copies = [
        pltpu.make_async_copy(part, out_ref.at[:, lanes], sems.at[i]) for i, (part, lanes) in enumerate(parts)
    ]
    for copy in copies:
        copy.start()
    for copy in copies:
        copy.wait()


def y_inverse_kernel(idx_ref, in_ref, table_ref, *refs):
    outs, (u_ref, t_ref, sems) = refs[:NREF], refs[NREF:]
    r = idx_ref[0]
    copies = [pltpu.make_async_copy(in_ref.at[:, x], u_ref.at[x], sems.at[x]) for x in range(XL)]
    for copy in copies:
        copy.start()
    for x in range(XL):
        copies[x].wait()
        t_ref[...] = left_multiply(table_ref[...], u_ref[x].reshape(N, 2 * KC))
        for s in range(NREF):
            start = pl.multiple_of(lax.rem(r + s, NREF) * 32, 32)
            outs[s][x] = t_ref[pl.ds(start, 32), :]


def gradient_kernel(shift_by, idx_ref, miller_ref, rho_ref, shift_ref, support_ref, *refs):
    ins, high_ref, low_ref = refs[:CH], refs[CH], refs[CH + 1]
    sums = refs[CH + 2 : -3]
    rho_out, shift_out, back_ref = refs[-3:]
    g = lax.rem(idx_ref[0] + NREF - shift_by, NREF)
    h, k, l = (miller_ref[c, g].astype(F32) for c in range(3))
    high, low = split(jnp.concatenate([ref[...].reshape(N, 2 * KC) for ref in ins], 1))
    dot = functools.partial(jnp.dot, preferred_element_type=F32)
    back_ref[...] = dot(high, high_ref[...]) + dot(low, high_ref[...]) + dot(high, low_ref[...])

    def step(x, carry):
        at = pl.ds(pl.multiple_of(x * 32, 32), 32)
        u = [shift_ref[c, x].astype(F32) for c in range(3)]
        mask = support_ref[x].astype(F32) * (1.0 / NREF)
        cosine, sine = cos_sin_turns(h * u[0] + k * u[1] + l * u[2])
        real, imag = back_ref[at, :N], back_ref[at, N:]
        p = mask * (cosine * real + sine * imag)
        q = mask * (cosine * imag - sine * real)
        twist = rho_ref[0, x].astype(F32) * q - rho_ref[1, x].astype(F32) * p
        for out, old, n, value in (
            (rho_out, 0, 0, p),
            (rho_out, 0, 1, q),
            (shift_out, 1, 0, h * twist),
            (shift_out, 1, 1, k * twist),
            (shift_out, 1, 2, l * twist),
        ):
            out[n, x] = sums[old][n, x] + value if sums else value
        return carry

    lax.fori_loop(0, XL, step, 0)


SMEM = pl.BlockSpec(memory_space=pltpu.SMEM)
VMEM = pl.BlockSpec(memory_space=pltpu.VMEM)
HBM = pl.BlockSpec(memory_space=pltpu.HBM)


def cost(flops, size):
    return pl.CostEstimate(flops=int(flops), bytes_accessed=int(size), transcendentals=0)


def f32(*shape):
    return jax.ShapeDtypeStruct(shape, F32)


def params(mib):
    return pltpu.CompilerParams(vmem_limit_bytes=mib * 1024 * 1024)


def hbm(*shape):
    return pltpu.HBM(shape, F32)


def in_hbm(value):
    return pltpu.with_memory_space_constraint(value, pltpu.HBM)


def after(value, *earlier):
    return lax.optimization_barrier((value, earlier))[0]


def head(c, millers, density, displacement, support):
    plane = lambda i: jnp.minimum(i, XL - 1)
    last = lambda i: jnp.maximum(i - 2, 0)
    return pl.pallas_call(
        head_kernel,
        grid=(XL + 2,),
        in_specs=[
            SMEM,
            pl.BlockSpec((2, 1, N, N), lambda i: (0, plane(i), 0, 0)),
            pl.BlockSpec((3, 1, N, N), lambda i: (0, plane(i), 0, 0)),
            pl.BlockSpec((1, N, N), lambda i: (plane(i), 0, 0)),
            pl.BlockSpec((6 * N, 2 * KC), lambda i: (0, c)),
            pl.BlockSpec((2 * N, 3 * N), lambda i: (0, 0)),
        ],
        out_specs=pl.BlockSpec((SLABS, 1, XL, 2 * KC), lambda i: (0, last(i), 0, 0)),
        out_shape=f32(SLABS, XL, XL, 2 * KC),
        scratch_shapes=[pltpu.VMEM((2, N, 2 * N), BF)] * 2 + [pltpu.VMEM((2, N, 2 * KC), BF)] * 2,
        compiler_params=params(60),
        cost_estimate=cost(6.4e9, 16e6),
        name=f"head_{c}",
    )(millers, density, displacement, support, jnp.asarray(right_forward()), jnp.asarray(left_table(False)))


def body(density, displacement, support, millers, amplitude):
    r = lax.axis_index("refl")
    idx = jnp.stack([r]).astype(jnp.int32)
    forward, inverse = jnp.asarray(left_table(False)), jnp.asarray(left_table(True))
    high, low = (jnp.asarray(t) for t in right_inverse())
    amp = amplitude.reshape(N * XL, N)
    millers = millers.T

    def x_both(c, part):
        return pl.pallas_call(
            x_kernel,
            grid=(1,),
            in_specs=[HBM, pl.BlockSpec((N * XL, KC), lambda i: (0, c)), VMEM, VMEM],
            out_specs=HBM,
            out_shape=hbm(N * XL, 2 * KC),
            scratch_shapes=[pltpu.VMEM((N * XL, KC), F32)] * 2 + [pltpu.SemaphoreType.DMA((2,))],
            compiler_params=params(24),
            cost_estimate=cost(6.4e9, 24e6),
            name=f"x_{c}",
        )(in_hbm(part.reshape(N * XL, 2 * KC)), amp, forward, inverse).reshape(SLABS, XL, XL, 2 * KC)

    def y_inverse(c, part):
        return pl.pallas_call(
            y_inverse_kernel,
            in_specs=[SMEM, HBM, VMEM],
            out_specs=[VMEM] * NREF,
            out_shape=[f32(XL, 32, 2 * KC)] * NREF,
            scratch_shapes=[
                pltpu.VMEM((XL, SLABS, XL, 2 * KC), F32),
                pltpu.VMEM((N, 2 * KC), F32),
                pltpu.SemaphoreType.DMA((XL,)),
            ],
            compiler_params=params(24),
            cost_estimate=cost(3.2e9, 12e6),
            name=f"y_inverse_{c}",
        )(idx, in_hbm(part), inverse)

    def over_grid(part):
        return lax.all_to_all(part, "grid", 0, 0, tiled=True)

    def over_refl(parts):
        ring = lambda s: [(i, (i + s) % NREF) for i in range(NREF)]
        moved = {s: lax.ppermute(parts[s], "refl", ring(s)) for s in R_ORDER}
        return [parts[0]] + [moved[s] for s in range(1, NREF)]

    def gradient(s, parts, sums):
        out_block = lambda n: pl.BlockSpec((n, XL, 32, N), lambda i, idx: (0, 0, 0, 0))
        whole = lambda i, idx: (0, 0)
        return tuple(
            pl.pallas_call(
                functools.partial(gradient_kernel, s),
                grid_spec=pltpu.PrefetchScalarGridSpec(
                    num_scalar_prefetch=1,
                    grid=(1,),
                    in_specs=[
                        SMEM,
                        pl.BlockSpec((2, XL, 32, N), lambda i, idx: (0, 0, idx[0], 0)),
                        pl.BlockSpec((3, XL, 32, N), lambda i, idx: (0, 0, idx[0], 0)),
                        pl.BlockSpec((XL, 32, N), lambda i, idx: (0, idx[0], 0)),
                    ]
                    + [pl.BlockSpec((XL, 32, 2 * KC), lambda i, idx: (0, 0, 0))] * CH
                    + [pl.BlockSpec((2 * N, 2 * N), whole)] * 2
                    + ([out_block(2), out_block(3)] if sums else []),
                    out_specs=[out_block(2), out_block(3)],
                    scratch_shapes=[pltpu.VMEM((N, 2 * N), F32)],
                ),
                out_shape=[f32(2, XL, 32, N), f32(3, XL, 32, N)],
                compiler_params=params(24),
                cost_estimate=cost(0.8e9, 5e6),
                name=f"gradient_{s}",
            )(idx, millers, density, displacement, support, *parts, high, low, *sums)
        )

    f0 = over_grid(head(0, millers, density, displacement, support))
    f1 = over_grid(after(head(1, millers, density, displacement, support), f0))
    b0 = over_grid(after(x_both(0, f0), f1))
    b1 = over_grid(after(x_both(1, f1), b0))
    r0 = over_refl(y_inverse(0, b0))
    r1 = over_refl(y_inverse(1, after(b1, *r0)))
    sums = ()
    for s in (0,) + R_ORDER:
        sums = gradient(s, (r0[s], r1[s]), sums)
    return sums


def solution(mesh):
    in_specs = (
        P(None, "grid", None, None),
        P(None, "grid", None, None),
        P("grid", None, None),
        P(),
        P("refl", None, "grid", None),
    )
    out_specs = (P(None, "grid", "refl", None), P(None, "grid", "refl", None))
    return jax.shard_map(body, mesh=mesh, in_specs=in_specs, out_specs=out_specs, check_vma=False)
```

```python
import functools
import math

import jax
import jax.numpy as jnp
import ml_dtypes
import numpy as np
from jax import lax
from jax.experimental import pallas as pl
from jax.experimental.pallas import tpu as pltpu
from jax.sharding import PartitionSpec as P

N = 256
CH = 2
KC = N // CH
SLABS = 32
XL = 8
NREF = 8
HEAD_ROWS = 32
R_ORDER = (5, 4, 1, 3, 7, 2, 6)
BF = jnp.bfloat16
F32 = jnp.float32


def split_np(table):
    high = table.astype(ml_dtypes.bfloat16)
    low = (table - high.astype(np.float64)).astype(ml_dtypes.bfloat16)
    return high, low


def dft_np():
    n = np.arange(N)
    angle = 2.0 * np.pi * (np.outer(n, n) % N) / N
    return np.cos(angle) / math.sqrt(N), -np.sin(angle) / math.sqrt(N)


def left_table(inverse):
    re, im = dft_np()
    high, low = split_np(np.concatenate([re, -im if inverse else im], 0))
    return np.concatenate([high, high, low], 1)


def packed_columns():
    chunk = np.arange(N) // KC
    inner = np.arange(N) % KC
    real = chunk * 2 * KC + inner
    return real, real + KC


def right_forward():
    re, im = dft_np()
    real, imag = packed_columns()
    table = np.zeros((2 * N, 2 * N))
    table[:N, real] = re
    table[:N, imag] = im
    table[N:, real] = -im
    table[N:, imag] = re
    high, low = split_np(table)
    return np.concatenate([high, high, low], 0)


def right_inverse():
    re, im = dft_np()
    real, imag = packed_columns()
    table = np.zeros((2 * N, 2 * N))
    table[real, :N] = re
    table[real, N:] = -im
    table[imag, :N] = im
    table[imag, N:] = re
    return split_np(table)


def sine_coefficients():
    b = 0.25 * np.cos((np.arange(400) + 0.5) / 400 * np.pi / 2)
    powers = np.stack([b ** (2 * k + 1) for k in range(6)], 1)
    return [float(v) for v in np.linalg.lstsq(powers, np.sin(2 * np.pi * b), rcond=None)[0]]


SINE = sine_coefficients()


def sine_turns(b):
    q = b * b
    acc = jnp.full_like(b, SINE[5])
    for k in range(4, -1, -1):
        acc = acc * q + SINE[k]
    return acc * b


def cos_sin_turns(t):
    t = t - jnp.round(t)
    cosine = sine_turns(0.25 - jnp.abs(t))
    u = t - 0.25
    u = u - jnp.round(u)
    return cosine, sine_turns(0.25 - jnp.abs(u))


def split(value):
    high = value.astype(BF)
    return high, (value - high.astype(F32)).astype(BF)


def left_multiply(table, packed):
    return left_split(table, *split(packed))


def left_split(table, high, low):
    both = jnp.dot(table, jnp.concatenate([high, low, high], 0), preferred_element_type=F32)
    real = both[:N, :KC] - both[N:, KC:]
    imag = both[:N, KC:] + both[N:, :KC]
    return jnp.concatenate([real, imag], 1)


def object_rows(hkl, rho_ref, shift_ref, support_ref, high_ref, low_ref, start, rows):
    at = pl.ds(start, rows)
    u = [shift_ref[c, 0, at, :].astype(F32) for c in range(3)]
    mask = support_ref[0, at, :].astype(F32)
    cosine, sine = cos_sin_turns(hkl[0] * u[0] + hkl[1] * u[1] + hkl[2] * u[2])
    real = mask * rho_ref[0, 0, at, :].astype(F32)
    imag = mask * rho_ref[1, 0, at, :].astype(F32)
    for part, value in enumerate((real * cosine - imag * sine, real * sine + imag * cosine)):
        high, low = split(value)
        high_ref[at, part * N : (part + 1) * N] = high
        low_ref[at, part * N : (part + 1) * N] = low


def head_kernel(miller_ref, rho_ref, shift_ref, support_ref, table_ref, left_ref, out_ref, high_ref, low_ref, ah_ref, al_ref):
    i = pl.program_id(0)
    r = lax.axis_index("refl")
    hkl = [miller_ref[c, r].astype(F32) for c in range(3)]
    now, before = lax.rem(i, 2), lax.rem(i + 1, 2)
    out_ref[:, 0] = left_split(left_ref[...], ah_ref[now], al_ref[now]).reshape(SLABS, XL, 2 * KC)
    high = high_ref[before]
    a = jnp.dot(jnp.concatenate([high, low_ref[before], high], 1), table_ref[...], preferred_element_type=F32)
    ah_ref[before], al_ref[before] = split(a)
    for row in range(0, N, HEAD_ROWS):
        object_rows(hkl, rho_ref, shift_ref, support_ref, high_ref.at[now], low_ref.at[now], row, HEAD_ROWS)


def x_kernel(in_ref, amp_ref, forward_ref, inverse_ref, *refs):
    out_ref, real_ref, imag_ref, sems = refs
    parts = ((real_ref, pl.ds(0, KC)), (imag_ref, pl.ds(KC, KC)))
    copies = [
        pltpu.make_async_copy(in_ref.at[:, lanes], part, sems.at[i]) for i, (part, lanes) in enumerate(parts)
    ]
    for copy in copies:
        copy.start()
    for copy in copies:
        copy.wait()

    def step(i, carry):
        at = pl.ds(i, N, stride=XL)
        spec = left_multiply(forward_ref[...], jnp.concatenate([real_ref[at, :], imag_ref[at, :]], 1))
        real, imag = spec[:, :KC], spec[:, KC:]
        ratio = amp_ref[at, :] * lax.rsqrt(jnp.maximum(real * real + imag * imag, 0.25))
        resid = jnp.concatenate([real - ratio * real, imag - ratio * imag], 1)
        back = left_multiply(inverse_ref[...], resid)
        real_ref[at, :] = back[:, :KC]
        imag_ref[at, :] = back[:, KC:]
        return carry

    lax.fori_loop(0, XL, step, 0)
    copies = [
        pltpu.make_async_copy(part, out_ref.at[:, lanes], sems.at[i]) for i, (part, lanes) in enumerate(parts)
    ]
    for copy in copies:
        copy.start()
    for copy in copies:
        copy.wait()


def partner(r, s, sign):
    return lax.rem(r // 2 + NREF // 2 + sign * (s // 2), NREF // 2) * 2 + lax.rem(r + s, 2)


def y_inverse_kernel(idx_ref, in_ref, table_ref, *refs):
    outs, t_ref = refs[:NREF], refs[NREF]
    r = idx_ref[0]

    def step(x, carry):
        t_ref[...] = left_multiply(table_ref[...], in_ref[:, x].reshape(N, 2 * KC))
        for s in range(NREF):
            start = pl.multiple_of(partner(r, s, 1) * 32, 32)
            outs[s][x] = t_ref[pl.ds(start, 32), :]
        return carry

    lax.fori_loop(0, XL, step, 0)


def gradient_kernel(shift_by, idx_ref, miller_ref, rho_ref, shift_ref, support_ref, *refs):
    ins, high_ref, low_ref = refs[:CH], refs[CH], refs[CH + 1]
    sums = refs[CH + 2 : -3]
    rho_out, shift_out, back_ref = refs[-3:]
    g = partner(idx_ref[0], shift_by, -1)
    h, k, l = (miller_ref[c, g].astype(F32) for c in range(3))
    high, low = split(jnp.concatenate([ref[...].reshape(N, 2 * KC) for ref in ins], 1))
    dot = functools.partial(jnp.dot, preferred_element_type=F32)
    back_ref[...] = dot(high, high_ref[...]) + dot(low, high_ref[...]) + dot(high, low_ref[...])

    def step(x, carry):
        at = pl.ds(pl.multiple_of(x * 32, 32), 32)
        u = [shift_ref[c, x].astype(F32) for c in range(3)]
        mask = support_ref[x].astype(F32) * (1.0 / NREF)
        cosine, sine = cos_sin_turns(h * u[0] + k * u[1] + l * u[2])
        real, imag = back_ref[at, :N], back_ref[at, N:]
        p = mask * (cosine * real + sine * imag)
        q = mask * (cosine * imag - sine * real)
        twist = rho_ref[0, x].astype(F32) * q - rho_ref[1, x].astype(F32) * p
        for out, old, n, value in (
            (rho_out, 0, 0, p),
            (rho_out, 0, 1, q),
            (shift_out, 1, 0, h * twist),
            (shift_out, 1, 1, k * twist),
            (shift_out, 1, 2, l * twist),
        ):
            out[n, x] = sums[old][n, x] + value if sums else value
        return carry

    lax.fori_loop(0, XL, step, 0)


SMEM = pl.BlockSpec(memory_space=pltpu.SMEM)
VMEM = pl.BlockSpec(memory_space=pltpu.VMEM)
HBM = pl.BlockSpec(memory_space=pltpu.HBM)


def cost(flops, size):
    return pl.CostEstimate(flops=int(flops), bytes_accessed=int(size), transcendentals=0)


def f32(*shape):
    return jax.ShapeDtypeStruct(shape, F32)


def params(mib):
    return pltpu.CompilerParams(vmem_limit_bytes=mib * 1024 * 1024)


def hbm(*shape):
    return pltpu.HBM(shape, F32)


def in_hbm(value):
    return pltpu.with_memory_space_constraint(value, pltpu.HBM)


def after(value, *earlier):
    return lax.optimization_barrier((value, earlier))[0]


def head(c, millers, density, displacement, support):
    plane = lambda i: jnp.minimum(i, XL - 1)
    last = lambda i: jnp.maximum(i - 2, 0)
    return pl.pallas_call(
        head_kernel,
        grid=(XL + 2,),
        in_specs=[
            SMEM,
            pl.BlockSpec((2, 1, N, N), lambda i: (0, plane(i), 0, 0)),
            pl.BlockSpec((3, 1, N, N), lambda i: (0, plane(i), 0, 0)),
            pl.BlockSpec((1, N, N), lambda i: (plane(i), 0, 0)),
            pl.BlockSpec((6 * N, 2 * KC), lambda i: (0, c)),
            pl.BlockSpec((2 * N, 3 * N), lambda i: (0, 0)),
        ],
        out_specs=pl.BlockSpec((SLABS, 1, XL, 2 * KC), lambda i: (0, last(i), 0, 0)),
        out_shape=f32(SLABS, XL, XL, 2 * KC),
        scratch_shapes=[pltpu.VMEM((2, N, 2 * N), BF)] * 2 + [pltpu.VMEM((2, N, 2 * KC), BF)] * 2,
        compiler_params=params(60),
        cost_estimate=cost(6.4e9, 16e6),
        name=f"head_{c}",
    )(millers, density, displacement, support, jnp.asarray(right_forward()), jnp.asarray(left_table(False)))


def body(density, displacement, support, millers, amplitude):
    r = lax.axis_index("refl")
    idx = jnp.stack([r]).astype(jnp.int32)
    forward, inverse = jnp.asarray(left_table(False)), jnp.asarray(left_table(True))
    high, low = (jnp.asarray(t) for t in right_inverse())
    amp = amplitude.reshape(N * XL, N)
    millers = millers.T

    def x_both(c, part):
        return pl.pallas_call(
            x_kernel,
            grid=(1,),
            in_specs=[HBM, pl.BlockSpec((N * XL, KC), lambda i: (0, c)), VMEM, VMEM],
            out_specs=HBM,
            out_shape=hbm(N * XL, 2 * KC),
            scratch_shapes=[pltpu.VMEM((N * XL, KC), F32)] * 2 + [pltpu.SemaphoreType.DMA((2,))],
            compiler_params=params(24),
            cost_estimate=cost(6.4e9, 24e6),
            name=f"x_{c}",
        )(in_hbm(part.reshape(N * XL, 2 * KC)), amp, forward, inverse).reshape(SLABS, XL, XL, 2 * KC)

    def y_inverse(c, part):
        return pl.pallas_call(
            y_inverse_kernel,
            in_specs=[SMEM, VMEM, VMEM],
            out_specs=[VMEM] * NREF,
            out_shape=[f32(XL, 32, 2 * KC)] * NREF,
            scratch_shapes=[pltpu.VMEM((N, 2 * KC), F32)],
            compiler_params=params(24),
            cost_estimate=cost(3.2e9, 12e6),
            name=f"y_inverse_{c}",
        )(idx, part, inverse)

    def over_grid(part):
        return lax.all_to_all(part, "grid", 0, 0, tiled=True)

    def over_refl(parts):
        ring = lambda s: [(i, (i // 2 + s // 2) % (NREF // 2) * 2 + (i + s) % 2) for i in range(NREF)]
        moved = {s: lax.ppermute(parts[s], "refl", ring(s)) for s in R_ORDER}
        return [parts[0]] + [moved[s] for s in range(1, NREF)]

    def gradient(s, parts, sums):
        out_block = lambda n: pl.BlockSpec((n, XL, 32, N), lambda i, idx: (0, 0, 0, 0))
        whole = lambda i, idx: (0, 0)
        return tuple(
            pl.pallas_call(
                functools.partial(gradient_kernel, s),
                grid_spec=pltpu.PrefetchScalarGridSpec(
                    num_scalar_prefetch=1,
                    grid=(1,),
                    in_specs=[
                        SMEM,
                        pl.BlockSpec((2, XL, 32, N), lambda i, idx: (0, 0, idx[0], 0)),
                        pl.BlockSpec((3, XL, 32, N), lambda i, idx: (0, 0, idx[0], 0)),
                        pl.BlockSpec((XL, 32, N), lambda i, idx: (0, idx[0], 0)),
                    ]
                    + [pl.BlockSpec((XL, 32, 2 * KC), lambda i, idx: (0, 0, 0))] * CH
                    + [pl.BlockSpec((2 * N, 2 * N), whole)] * 2
                    + ([out_block(2), out_block(3)] if sums else []),
                    out_specs=[out_block(2), out_block(3)],
                    scratch_shapes=[pltpu.VMEM((N, 2 * N), F32)],
                ),
                out_shape=[f32(2, XL, 32, N), f32(3, XL, 32, N)],
                compiler_params=params(24),
                cost_estimate=cost(0.8e9, 5e6),
                name=f"gradient_{s}",
            )(idx, millers, density, displacement, support, *parts, high, low, *sums)
        )

    f0 = over_grid(head(0, millers, density, displacement, support))
    f1 = over_grid(after(head(1, millers, density, displacement, support), f0))
    b0 = over_grid(after(x_both(0, f0), f1))
    b1 = over_grid(after(x_both(1, f1), b0))
    r0 = over_refl(y_inverse(0, in_hbm(b0)))
    r1 = over_refl(y_inverse(1, after(b1, *r0)))
    sums = ()
    for s in (0,) + R_ORDER:
        sums = gradient(s, (r0[s], r1[s]), sums)
    return sums


def solution(mesh):
    in_specs = (
        P(None, "grid", None, None),
        P(None, "grid", None, None),
        P("grid", None, None),
        P(),
        P("refl", None, "grid", None),
    )
    out_specs = (P(None, "grid", "refl", None), P(None, "grid", "refl", None))
    return jax.shard_map(body, mesh=mesh, in_specs=in_specs, out_specs=out_specs, check_vma=False)
```

```python
import functools
import math

import jax
import jax.numpy as jnp
import ml_dtypes
import numpy as np
from jax import lax
from jax.experimental import pallas as pl
from jax.experimental.pallas import tpu as pltpu
from jax.sharding import PartitionSpec as P

N = 256
CH = 2
KC = N // CH
SLABS = 32
XL = 8
NREF = 8
HEAD_ROWS = 32
R_ORDER = (5, 4, 1, 3, 7, 2, 6)
BF = jnp.bfloat16
F32 = jnp.float32


def split_np(table):
    high = table.astype(ml_dtypes.bfloat16)
    low = (table - high.astype(np.float64)).astype(ml_dtypes.bfloat16)
    return high, low


def dft_np():
    n = np.arange(N)
    angle = 2.0 * np.pi * (np.outer(n, n) % N) / N
    return np.cos(angle) / math.sqrt(N), -np.sin(angle) / math.sqrt(N)


def left_table(inverse):
    re, im = dft_np()
    high, low = split_np(np.concatenate([re, -im if inverse else im], 0))
    return np.concatenate([high, high, low], 1)


def packed_columns():
    chunk = np.arange(N) // KC
    inner = np.arange(N) % KC
    real = chunk * 2 * KC + inner
    return real, real + KC


def right_forward():
    re, im = dft_np()
    real, imag = packed_columns()
    table = np.zeros((2 * N, 2 * N))
    table[:N, real] = re
    table[:N, imag] = im
    table[N:, real] = -im
    table[N:, imag] = re
    high, low = split_np(table)
    return np.concatenate([high, high, low], 0)


def right_inverse():
    re, im = dft_np()
    real, imag = packed_columns()
    table = np.zeros((2 * N, 2 * N))
    table[real, :N] = re
    table[real, N:] = -im
    table[imag, :N] = im
    table[imag, N:] = re
    high, low = split_np(table)
    return np.concatenate([high, high, low], 0)


def sine_coefficients():
    b = 0.25 * np.cos((np.arange(400) + 0.5) / 400 * np.pi / 2)
    powers = np.stack([b ** (2 * k + 1) for k in range(6)], 1)
    return [float(v) for v in np.linalg.lstsq(powers, np.sin(2 * np.pi * b), rcond=None)[0]]


SINE = sine_coefficients()


def sine_turns(b):
    q = b * b
    acc = jnp.full_like(b, SINE[5])
    for k in range(4, -1, -1):
        acc = acc * q + SINE[k]
    return acc * b


def cos_sin_turns(t):
    t = t - jnp.round(t)
    cosine = sine_turns(0.25 - jnp.abs(t))
    u = t - 0.25
    u = u - jnp.round(u)
    return cosine, sine_turns(0.25 - jnp.abs(u))


def split(value):
    high = value.astype(BF)
    return high, (value - high.astype(F32)).astype(BF)


def left_multiply(table, packed):
    return left_split(table, *split(packed))


def left_split(table, high, low):
    both = jnp.dot(table, jnp.concatenate([high, low, high], 0), preferred_element_type=F32)
    real = both[:N, :KC] - both[N:, KC:]
    imag = both[:N, KC:] + both[N:, :KC]
    return jnp.concatenate([real, imag], 1)


def object_rows(hkl, rho_ref, shift_ref, support_ref, high_ref, low_ref, start, rows):
    at = pl.ds(start, rows)
    u = [shift_ref[c, 0, at, :].astype(F32) for c in range(3)]
    mask = support_ref[0, at, :].astype(F32)
    cosine, sine = cos_sin_turns(hkl[0] * u[0] + hkl[1] * u[1] + hkl[2] * u[2])
    real = mask * rho_ref[0, 0, at, :].astype(F32)
    imag = mask * rho_ref[1, 0, at, :].astype(F32)
    for part, value in enumerate((real * cosine - imag * sine, real * sine + imag * cosine)):
        high, low = split(value)
        high_ref[at, part * N : (part + 1) * N] = high
        low_ref[at, part * N : (part + 1) * N] = low


def head_kernel(miller_ref, rho_ref, shift_ref, support_ref, table_ref, left_ref, out_ref, high_ref, low_ref, ah_ref, al_ref):
    i = pl.program_id(0)
    r = lax.axis_index("refl")
    hkl = [miller_ref[c, r].astype(F32) for c in range(3)]
    now, before = lax.rem(i, 2), lax.rem(i + 1, 2)
    out_ref[:, 0] = left_split(left_ref[...], ah_ref[now], al_ref[now]).reshape(SLABS, XL, 2 * KC)
    high = high_ref[before]
    a = jnp.dot(jnp.concatenate([high, low_ref[before], high], 1), table_ref[...], preferred_element_type=F32)
    ah_ref[before], al_ref[before] = split(a)
    for row in range(0, N, HEAD_ROWS):
        object_rows(hkl, rho_ref, shift_ref, support_ref, high_ref.at[now], low_ref.at[now], row, HEAD_ROWS)


def x_kernel(in_ref, amp_ref, forward_ref, inverse_ref, *refs):
    out_ref, real_ref, imag_ref, sems = refs
    parts = ((real_ref, pl.ds(0, KC)), (imag_ref, pl.ds(KC, KC)))
    copies = [
        pltpu.make_async_copy(in_ref.at[:, lanes], part, sems.at[i]) for i, (part, lanes) in enumerate(parts)
    ]
    for copy in copies:
        copy.start()
    for copy in copies:
        copy.wait()

    def step(i, carry):
        at = pl.ds(i, N, stride=XL)
        spec = left_multiply(forward_ref[...], jnp.concatenate([real_ref[at, :], imag_ref[at, :]], 1))
        real, imag = spec[:, :KC], spec[:, KC:]
        ratio = amp_ref[at, :] * lax.rsqrt(jnp.maximum(real * real + imag * imag, 0.25))
        resid = jnp.concatenate([real - ratio * real, imag - ratio * imag], 1)
        back = left_multiply(inverse_ref[...], resid)
        real_ref[at, :] = back[:, :KC]
        imag_ref[at, :] = back[:, KC:]
        return carry

    lax.fori_loop(0, XL, step, 0)
    copies = [
        pltpu.make_async_copy(part, out_ref.at[:, lanes], sems.at[i]) for i, (part, lanes) in enumerate(parts)
    ]
    for copy in copies:
        copy.start()
    for copy in copies:
        copy.wait()


def partner(r, s, sign):
    return lax.rem(r // 2 + NREF // 2 + sign * (s // 2), NREF // 2) * 2 + lax.rem(r + s, 2)


def y_inverse_kernel(idx_ref, in_ref, table_ref, *refs):
    outs, t_ref = refs[:NREF], refs[NREF]
    t_ref[...] = left_multiply(table_ref[...], in_ref[:, 0].reshape(N, 2 * KC))
    for s in range(NREF):
        start = pl.multiple_of(partner(idx_ref[0], s, 1) * 32, 32)
        outs[s][0] = t_ref[pl.ds(start, 32), :]


def gradient_kernel(shift_by, idx_ref, miller_ref, rho_ref, shift_ref, support_ref, *refs):
    ins, table_ref, sums = refs[:CH], refs[CH], refs[CH + 1 : -2]
    rho_out, shift_out = refs[-2:]
    g = partner(idx_ref[0], shift_by, -1)
    h, k, l = (miller_ref[c, g].astype(F32) for c in range(3))
    rows = pl.ds(pl.multiple_of(idx_ref[0] * 32, 32), 32)
    half = XL // 2
    backs = []
    for first in (0, half):
        packed = [ref[first : first + half].reshape(half * 32, 2 * KC) for ref in ins]
        high, low = split(jnp.concatenate(packed, 1))
        backs.append(
            jnp.dot(jnp.concatenate([high, low, high], 1), table_ref[...], preferred_element_type=F32)
        )
    for x in range(XL):
        back = backs[x // half][x % half * 32 : (x % half + 1) * 32]
        u = [shift_ref[c, x, rows, :].astype(F32) for c in range(3)]
        mask = support_ref[x, rows, :].astype(F32) * (1.0 / NREF)
        cosine, sine = cos_sin_turns(h * u[0] + k * u[1] + l * u[2])
        real, imag = back[:, :N], back[:, N:]
        p = mask * (cosine * real + sine * imag)
        q = mask * (cosine * imag - sine * real)
        twist = rho_ref[0, x, rows, :].astype(F32) * q - rho_ref[1, x, rows, :].astype(F32) * p
        for out, old, n, value in (
            (rho_out, 0, 0, p),
            (rho_out, 0, 1, q),
            (shift_out, 1, 0, h * twist),
            (shift_out, 1, 1, k * twist),
            (shift_out, 1, 2, l * twist),
        ):
            out[n, x] = sums[old][n, x] + value if sums else value


SMEM = pl.BlockSpec(memory_space=pltpu.SMEM)
VMEM = pl.BlockSpec(memory_space=pltpu.VMEM)
HBM = pl.BlockSpec(memory_space=pltpu.HBM)


def cost(flops, size):
    return pl.CostEstimate(flops=int(flops), bytes_accessed=int(size), transcendentals=0)


def f32(*shape):
    return jax.ShapeDtypeStruct(shape, F32)


def params(mib):
    return pltpu.CompilerParams(vmem_limit_bytes=mib * 1024 * 1024)


def hbm(*shape):
    return pltpu.HBM(shape, F32)


def in_hbm(value):
    return pltpu.with_memory_space_constraint(value, pltpu.HBM)


def after(value, *earlier):
    return lax.optimization_barrier((value, earlier))[0]


def head(c, millers, density, displacement, support):
    plane = lambda i: jnp.minimum(i, XL - 1)
    last = lambda i: jnp.maximum(i - 2, 0)
    return pl.pallas_call(
        head_kernel,
        grid=(XL + 2,),
        in_specs=[
            SMEM,
            pl.BlockSpec((2, 1, N, N), lambda i: (0, plane(i), 0, 0)),
            pl.BlockSpec((3, 1, N, N), lambda i: (0, plane(i), 0, 0)),
            pl.BlockSpec((1, N, N), lambda i: (plane(i), 0, 0)),
            pl.BlockSpec((6 * N, 2 * KC), lambda i: (0, c)),
            pl.BlockSpec((2 * N, 3 * N), lambda i: (0, 0)),
        ],
        out_specs=pl.BlockSpec((SLABS, 1, XL, 2 * KC), lambda i: (0, last(i), 0, 0)),
        out_shape=f32(SLABS, XL, XL, 2 * KC),
        scratch_shapes=[pltpu.VMEM((2, N, 2 * N), BF)] * 2 + [pltpu.VMEM((2, N, 2 * KC), BF)] * 2,
        compiler_params=params(60),
        cost_estimate=cost(6.4e9, 16e6),
        name=f"head_{c}",
    )(millers, density, displacement, support, jnp.asarray(right_forward()), jnp.asarray(left_table(False)))


def body(density, displacement, support, millers, amplitude):
    r = lax.axis_index("refl")
    idx = jnp.stack([r]).astype(jnp.int32)
    forward, inverse = jnp.asarray(left_table(False)), jnp.asarray(left_table(True))
    last_table = jnp.asarray(right_inverse())
    amp = amplitude.reshape(N * XL, N)
    millers = millers.T

    def x_both(c, part):
        return pl.pallas_call(
            x_kernel,
            grid=(1,),
            in_specs=[HBM, pl.BlockSpec((N * XL, KC), lambda i: (0, c)), VMEM, VMEM],
            out_specs=HBM,
            out_shape=hbm(N * XL, 2 * KC),
            scratch_shapes=[pltpu.VMEM((N * XL, KC), F32)] * 2 + [pltpu.SemaphoreType.DMA((2,))],
            compiler_params=params(24),
            cost_estimate=cost(6.4e9, 24e6),
            name=f"x_{c}",
        )(in_hbm(part.reshape(N * XL, 2 * KC)), amp, forward, inverse).reshape(SLABS, XL, XL, 2 * KC)

    def y_inverse(c, part):
        return pl.pallas_call(
            y_inverse_kernel,
            grid=(XL,),
            in_specs=[
                SMEM,
                pl.BlockSpec((SLABS, 1, XL, 2 * KC), lambda x: (0, x, 0, 0)),
                pl.BlockSpec((2 * N, 3 * N), lambda x: (0, 0)),
            ],
            out_specs=[pl.BlockSpec((1, 32, 2 * KC), lambda x: (x, 0, 0))] * NREF,
            out_shape=[f32(XL, 32, 2 * KC)] * NREF,
            scratch_shapes=[pltpu.VMEM((N, 2 * KC), F32)],
            compiler_params=params(24),
            cost_estimate=cost(3.2e9, 12e6),
            name=f"y_inverse_{c}",
        )(idx, in_hbm(part), inverse)

    def over_grid(part):
        return lax.all_to_all(part, "grid", 0, 0, tiled=True)

    def over_refl(parts):
        ring = lambda s: [(i, (i // 2 + s // 2) % (NREF // 2) * 2 + (i + s) % 2) for i in range(NREF)]
        moved = {s: lax.ppermute(parts[s], "refl", ring(s)) for s in R_ORDER}
        return [parts[0]] + [moved[s] for s in range(1, NREF)]

    def gradient(s, parts, sums):
        return tuple(
            pl.pallas_call(
                functools.partial(gradient_kernel, s),
                in_specs=[SMEM, SMEM] + [VMEM] * (3 + CH + 1 + len(sums)),
                out_specs=[VMEM] * 2,
                out_shape=[f32(2, XL, 32, N), f32(3, XL, 32, N)],
                compiler_params=params(16),
                cost_estimate=cost(0.8e9, 5e6),
                name=f"gradient_{s}",
            )(idx, millers, density, displacement, support, *parts, last_table, *sums)
        )

    f0 = over_grid(head(0, millers, density, displacement, support))
    f1 = over_grid(after(head(1, millers, density, displacement, support), f0))
    b0 = over_grid(after(x_both(0, f0), f1))
    b1 = over_grid(after(x_both(1, f1), b0))
    r0 = over_refl(y_inverse(0, b0))
    r1 = over_refl(y_inverse(1, after(b1, *r0)))
    sums = ()
    for s in (0,) + R_ORDER:
        sums = gradient(s, (r0[s], r1[s]), sums)
    return sums


def solution(mesh):
    in_specs = (
        P(None, "grid", None, None),
        P(None, "grid", None, None),
        P("grid", None, None),
        P(),
        P("refl", None, "grid", None),
    )
    out_specs = (P(None, "grid", "refl", None), P(None, "grid", "refl", None))
    return jax.shard_map(body, mesh=mesh, in_specs=in_specs, out_specs=out_specs, check_vma=False)
```

```python
import functools
import math

import jax
import jax.numpy as jnp
import ml_dtypes
import numpy as np
from jax import lax
from jax.experimental import pallas as pl
from jax.experimental.pallas import tpu as pltpu
from jax.sharding import PartitionSpec as P

N = 256
CH = 2
KC = N // CH
SLABS = 32
XL = 8
NREF = 8
HEAD_ROWS = 32
R_ORDER = (4, 5, 3, 2, 7, 6, 1)
BF = jnp.bfloat16
F32 = jnp.float32


def split_np(table):
    high = table.astype(ml_dtypes.bfloat16)
    low = (table - high.astype(np.float64)).astype(ml_dtypes.bfloat16)
    return high, low


def dft_np():
    n = np.arange(N)
    angle = 2.0 * np.pi * (np.outer(n, n) % N) / N
    return np.cos(angle) / math.sqrt(N), -np.sin(angle) / math.sqrt(N)


def left_table(inverse):
    re, im = dft_np()
    high, low = split_np(np.concatenate([re, -im if inverse else im], 0))
    return np.concatenate([high, high, low], 1)


def packed_columns():
    chunk = np.arange(N) // KC
    inner = np.arange(N) % KC
    real = chunk * 2 * KC + inner
    return real, real + KC


def right_forward():
    re, im = dft_np()
    real, imag = packed_columns()
    table = np.zeros((2 * N, 2 * N))
    table[:N, real] = re
    table[:N, imag] = im
    table[N:, real] = -im
    table[N:, imag] = re
    high, low = split_np(table)
    return np.concatenate([high, high, low], 0)


def right_inverse():
    re, im = dft_np()
    real, imag = packed_columns()
    table = np.zeros((2 * N, 2 * N))
    table[real, :N] = re
    table[real, N:] = -im
    table[imag, :N] = im
    table[imag, N:] = re
    high, low = split_np(table)
    return np.concatenate([high, high, low], 0)


def sine_coefficients():
    b = 0.25 * np.cos((np.arange(400) + 0.5) / 400 * np.pi / 2)
    powers = np.stack([b ** (2 * k + 1) for k in range(6)], 1)
    return [float(v) for v in np.linalg.lstsq(powers, np.sin(2 * np.pi * b), rcond=None)[0]]


SINE = sine_coefficients()


def sine_turns(b):
    q = b * b
    acc = jnp.full_like(b, SINE[5])
    for k in range(4, -1, -1):
        acc = acc * q + SINE[k]
    return acc * b


def cos_sin_turns(t):
    t = t - jnp.round(t)
    cosine = sine_turns(0.25 - jnp.abs(t))
    u = t - 0.25
    u = u - jnp.round(u)
    return cosine, sine_turns(0.25 - jnp.abs(u))


def split(value):
    high = value.astype(BF)
    return high, (value - high.astype(F32)).astype(BF)


def left_multiply(table, packed):
    return left_split(table, *split(packed))


def left_split(table, high, low):
    both = jnp.dot(table, jnp.concatenate([high, low, high], 0), preferred_element_type=F32)
    real = both[:N, :KC] - both[N:, KC:]
    imag = both[:N, KC:] + both[N:, :KC]
    return jnp.concatenate([real, imag], 1)


def object_rows(hkl, rho_ref, shift_ref, support_ref, high_ref, low_ref, start, rows):
    at = pl.ds(start, rows)
    u = [shift_ref[c, 0, at, :].astype(F32) for c in range(3)]
    mask = support_ref[0, at, :].astype(F32)
    cosine, sine = cos_sin_turns(hkl[0] * u[0] + hkl[1] * u[1] + hkl[2] * u[2])
    real = mask * rho_ref[0, 0, at, :].astype(F32)
    imag = mask * rho_ref[1, 0, at, :].astype(F32)
    for part, value in enumerate((real * cosine - imag * sine, real * sine + imag * cosine)):
        high, low = split(value)
        high_ref[at, part * N : (part + 1) * N] = high
        low_ref[at, part * N : (part + 1) * N] = low


def head_kernel(miller_ref, rho_ref, shift_ref, support_ref, table_ref, left_ref, out_ref, high_ref, low_ref, ah_ref, al_ref):
    i = pl.program_id(0)
    r = lax.axis_index("refl")
    hkl = [miller_ref[c, r].astype(F32) for c in range(3)]
    now, before = lax.rem(i, 2), lax.rem(i + 1, 2)
    out_ref[:, 0] = left_split(left_ref[...], ah_ref[now], al_ref[now]).reshape(SLABS, XL, 2 * KC)
    high = high_ref[before]
    a = jnp.dot(jnp.concatenate([high, low_ref[before], high], 1), table_ref[...], preferred_element_type=F32)
    ah_ref[before], al_ref[before] = split(a)
    for row in range(0, N, HEAD_ROWS):
        object_rows(hkl, rho_ref, shift_ref, support_ref, high_ref.at[now], low_ref.at[now], row, HEAD_ROWS)


def x_kernel(in_ref, amp_ref, forward_ref, inverse_ref, *refs):
    out_ref, real_ref, imag_ref, sems = refs
    parts = ((real_ref, pl.ds(0, KC)), (imag_ref, pl.ds(KC, KC)))
    copies = [
        pltpu.make_async_copy(in_ref.at[:, lanes], part, sems.at[i]) for i, (part, lanes) in enumerate(parts)
    ]
    for copy in copies:
        copy.start()
    for copy in copies:
        copy.wait()

    def step(i, carry):
        at = pl.ds(i, N, stride=XL)
        spec = left_multiply(forward_ref[...], jnp.concatenate([real_ref[at, :], imag_ref[at, :]], 1))
        real, imag = spec[:, :KC], spec[:, KC:]
        ratio = amp_ref[at, :] * lax.rsqrt(jnp.maximum(real * real + imag * imag, 0.25))
        resid = jnp.concatenate([real - ratio * real, imag - ratio * imag], 1)
        back = left_multiply(inverse_ref[...], resid)
        real_ref[at, :] = back[:, :KC]
        imag_ref[at, :] = back[:, KC:]
        return carry

    lax.fori_loop(0, XL, step, 0)
    copies = [
        pltpu.make_async_copy(part, out_ref.at[:, lanes], sems.at[i]) for i, (part, lanes) in enumerate(parts)
    ]
    for copy in copies:
        copy.start()
    for copy in copies:
        copy.wait()


def partner(r, s, sign):
    return lax.rem(r // 2 + NREF // 2 + sign * (s // 2), NREF // 2) * 2 + lax.rem(r + s, 2)


def y_inverse_kernel(idx_ref, in_ref, table_ref, *refs):
    outs, t_ref = refs[:NREF], refs[NREF]
    r = idx_ref[0]

    def step(x, carry):
        t_ref[...] = left_multiply(table_ref[...], in_ref[:, x].reshape(N, 2 * KC))
        for s in range(NREF):
            start = pl.multiple_of(partner(r, s, 1) * 32, 32)
            outs[s][x] = t_ref[pl.ds(start, 32), :]
        return carry

    lax.fori_loop(0, XL, step, 0)


def gradient_kernel(shift_by, idx_ref, miller_ref, rho_ref, shift_ref, support_ref, *refs):
    ins, table_ref, sums = refs[:CH], refs[CH], refs[CH + 1 : -2]
    rho_out, shift_out = refs[-2:]
    g = partner(idx_ref[0], shift_by, -1)
    h, k, l = (miller_ref[c, g].astype(F32) for c in range(3))
    rows = pl.ds(pl.multiple_of(idx_ref[0] * 32, 32), 32)
    half = XL // 2
    backs = []
    for first in (0, half):
        packed = [ref[first : first + half].reshape(half * 32, 2 * KC) for ref in ins]
        high, low = split(jnp.concatenate(packed, 1))
        backs.append(
            jnp.dot(jnp.concatenate([high, low, high], 1), table_ref[...], preferred_element_type=F32)
        )
    for x in range(XL):
        back = backs[x // half][x % half * 32 : (x % half + 1) * 32]
        u = [shift_ref[c, x, rows, :].astype(F32) for c in range(3)]
        mask = support_ref[x, rows, :].astype(F32) * (1.0 / NREF)
        cosine, sine = cos_sin_turns(h * u[0] + k * u[1] + l * u[2])
        real, imag = back[:, :N], back[:, N:]
        p = mask * (cosine * real + sine * imag)
        q = mask * (cosine * imag - sine * real)
        twist = rho_ref[0, x, rows, :].astype(F32) * q - rho_ref[1, x, rows, :].astype(F32) * p
        for out, old, n, value in (
            (rho_out, 0, 0, p),
            (rho_out, 0, 1, q),
            (shift_out, 1, 0, h * twist),
            (shift_out, 1, 1, k * twist),
            (shift_out, 1, 2, l * twist),
        ):
            out[n, x] = sums[old][n, x] + value if sums else value


SMEM = pl.BlockSpec(memory_space=pltpu.SMEM)
VMEM = pl.BlockSpec(memory_space=pltpu.VMEM)
HBM = pl.BlockSpec(memory_space=pltpu.HBM)


def cost(flops, size):
    return pl.CostEstimate(flops=int(flops), bytes_accessed=int(size), transcendentals=0)


def f32(*shape):
    return jax.ShapeDtypeStruct(shape, F32)


def params(mib):
    return pltpu.CompilerParams(vmem_limit_bytes=mib * 1024 * 1024)


def hbm(*shape):
    return pltpu.HBM(shape, F32)


def in_hbm(value):
    return pltpu.with_memory_space_constraint(value, pltpu.HBM)


def after(value, *earlier):
    return lax.optimization_barrier((value, earlier))[0]


def head(c, millers, density, displacement, support):
    plane = lambda i: jnp.minimum(i, XL - 1)
    last = lambda i: jnp.maximum(i - 2, 0)
    return pl.pallas_call(
        head_kernel,
        grid=(XL + 2,),
        in_specs=[
            SMEM,
            pl.BlockSpec((2, 1, N, N), lambda i: (0, plane(i), 0, 0)),
            pl.BlockSpec((3, 1, N, N), lambda i: (0, plane(i), 0, 0)),
            pl.BlockSpec((1, N, N), lambda i: (plane(i), 0, 0)),
            pl.BlockSpec((6 * N, 2 * KC), lambda i: (0, c)),
            pl.BlockSpec((2 * N, 3 * N), lambda i: (0, 0)),
        ],
        out_specs=pl.BlockSpec((SLABS, 1, XL, 2 * KC), lambda i: (0, last(i), 0, 0)),
        out_shape=f32(SLABS, XL, XL, 2 * KC),
        scratch_shapes=[pltpu.VMEM((2, N, 2 * N), BF)] * 2 + [pltpu.VMEM((2, N, 2 * KC), BF)] * 2,
        compiler_params=params(60),
        cost_estimate=cost(6.4e9, 16e6),
        name=f"head_{c}",
    )(millers, density, displacement, support, jnp.asarray(right_forward()), jnp.asarray(left_table(False)))


def body(density, displacement, support, millers, amplitude):
    r = lax.axis_index("refl")
    idx = jnp.stack([r]).astype(jnp.int32)
    forward, inverse = jnp.asarray(left_table(False)), jnp.asarray(left_table(True))
    last_table = jnp.asarray(right_inverse())
    amp = amplitude.reshape(N * XL, N)
    millers = millers.T

    def x_both(c, part):
        return pl.pallas_call(
            x_kernel,
            grid=(1,),
            in_specs=[HBM, pl.BlockSpec((N * XL, KC), lambda i: (0, c)), VMEM, VMEM],
            out_specs=HBM,
            out_shape=hbm(N * XL, 2 * KC),
            scratch_shapes=[pltpu.VMEM((N * XL, KC), F32)] * 2 + [pltpu.SemaphoreType.DMA((2,))],
            compiler_params=params(24),
            cost_estimate=cost(6.4e9, 24e6),
            name=f"x_{c}",
        )(in_hbm(part.reshape(N * XL, 2 * KC)), amp, forward, inverse).reshape(SLABS, XL, XL, 2 * KC)

    def y_inverse(c, part):
        return pl.pallas_call(
            y_inverse_kernel,
            in_specs=[SMEM, VMEM, VMEM],
            out_specs=[VMEM] * NREF,
            out_shape=[f32(XL, 32, 2 * KC)] * NREF,
            scratch_shapes=[pltpu.VMEM((N, 2 * KC), F32)],
            compiler_params=params(24),
            cost_estimate=cost(3.2e9, 12e6),
            name=f"y_inverse_{c}",
        )(idx, part, in_hbm(inverse))

    def over_grid(part):
        return lax.all_to_all(part, "grid", 0, 0, tiled=True)

    def over_refl(parts, order):
        ring = lambda s: [(i, (i // 2 + s // 2) % (NREF // 2) * 2 + (i + s) % 2) for i in range(NREF)]
        moved = {s: lax.ppermute(parts[s], "refl", ring(s)) for s in order}
        return [parts[0]] + [moved[s] for s in range(1, NREF)]

    def gradient(s, parts, sums):
        return tuple(
            pl.pallas_call(
                functools.partial(gradient_kernel, s),
                in_specs=[SMEM, SMEM] + [VMEM] * (3 + CH + 1 + len(sums)),
                out_specs=[VMEM] * 2,
                out_shape=[f32(2, XL, 32, N), f32(3, XL, 32, N)],
                compiler_params=params(16),
                cost_estimate=cost(0.8e9, 5e6),
                name=f"gradient_{s}",
            )(idx, millers, density, displacement, support, *parts, last_table, *sums)
        )

    f0 = over_grid(head(0, millers, density, displacement, support))
    f1 = over_grid(after(head(1, millers, density, displacement, support), f0))
    b0 = over_grid(after(x_both(0, f0), f1))
    b1 = over_grid(after(x_both(1, f1), b0))
    r0 = over_refl(y_inverse(0, in_hbm(b0)), (5, 4, 1, 3, 7, 2, 6))
    r1 = over_refl(y_inverse(1, after(b1, *r0)), R_ORDER)
    sums = ()
    for s in (0,) + R_ORDER:
        sums = gradient(s, (r0[s], r1[s]), sums)
    return sums


def solution(mesh):
    in_specs = (
        P(None, "grid", None, None),
        P(None, "grid", None, None),
        P("grid", None, None),
        P(),
        P("refl", None, "grid", None),
    )
    out_specs = (P(None, "grid", "refl", None), P(None, "grid", "refl", None))
    return jax.shard_map(body, mesh=mesh, in_specs=in_specs, out_specs=out_specs, check_vma=False)
```

```python
import functools
import math

import jax
import jax.numpy as jnp
import ml_dtypes
import numpy as np
from jax import lax
from jax.experimental import pallas as pl
from jax.experimental.pallas import tpu as pltpu
from jax.sharding import PartitionSpec as P

N = 256
CH = 2
KC = N // CH
SLABS = 32
XL = 8
NREF = 8
HEAD_ROWS = 32
R_ORDER = (5, 4, 1, 3, 7, 2, 6)
BF = jnp.bfloat16
F32 = jnp.float32


def split_np(table):
    high = table.astype(ml_dtypes.bfloat16)
    low = (table - high.astype(np.float64)).astype(ml_dtypes.bfloat16)
    return high, low


def dft_np():
    n = np.arange(N)
    angle = 2.0 * np.pi * (np.outer(n, n) % N) / N
    return np.cos(angle) / math.sqrt(N), -np.sin(angle) / math.sqrt(N)


def left_table(inverse):
    re, im = dft_np()
    high, low = split_np(np.concatenate([re, -im if inverse else im], 0))
    return np.concatenate([high, high, low], 1)


def packed_columns():
    chunk = np.arange(N) // KC
    inner = np.arange(N) % KC
    real = chunk * 2 * KC + inner
    return real, real + KC


def right_forward():
    re, im = dft_np()
    real, imag = packed_columns()
    table = np.zeros((2 * N, 2 * N))
    table[:N, real] = re
    table[:N, imag] = im
    table[N:, real] = -im
    table[N:, imag] = re
    high, low = split_np(table)
    return np.concatenate([high, high, low], 0)


def right_inverse():
    re, im = dft_np()
    real, imag = packed_columns()
    table = np.zeros((2 * N, 2 * N))
    table[real, :N] = re
    table[real, N:] = -im
    table[imag, :N] = im
    table[imag, N:] = re
    high, low = split_np(table)
    return np.concatenate([high, high, low], 0)


def sine_coefficients():
    b = 0.25 * np.cos((np.arange(400) + 0.5) / 400 * np.pi / 2)
    powers = np.stack([b ** (2 * k + 1) for k in range(6)], 1)
    return [float(v) for v in np.linalg.lstsq(powers, np.sin(2 * np.pi * b), rcond=None)[0]]


SINE = sine_coefficients()


def sine_turns(b):
    q = b * b
    acc = jnp.full_like(b, SINE[5])
    for k in range(4, -1, -1):
        acc = acc * q + SINE[k]
    return acc * b


def cos_sin_turns(t):
    t = t - jnp.round(t)
    cosine = sine_turns(0.25 - jnp.abs(t))
    u = t - 0.25
    u = u - jnp.round(u)
    return cosine, sine_turns(0.25 - jnp.abs(u))


def split(value):
    high = value.astype(BF)
    return high, (value - high.astype(F32)).astype(BF)


def left_multiply(table, packed):
    return left_split(table, *split(packed))


def left_split(table, high, low):
    both = jnp.dot(table, jnp.concatenate([high, low, high], 0), preferred_element_type=F32)
    real = both[:N, :KC] - both[N:, KC:]
    imag = both[:N, KC:] + both[N:, :KC]
    return jnp.concatenate([real, imag], 1)


def object_rows(hkl, rho_ref, shift_ref, support_ref, high_ref, low_ref, start, rows):
    at = pl.ds(start, rows)
    u = [shift_ref[c, 0, at, :].astype(F32) for c in range(3)]
    mask = support_ref[0, at, :].astype(F32)
    cosine, sine = cos_sin_turns(hkl[0] * u[0] + hkl[1] * u[1] + hkl[2] * u[2])
    real = mask * rho_ref[0, 0, at, :].astype(F32)
    imag = mask * rho_ref[1, 0, at, :].astype(F32)
    for part, value in enumerate((real * cosine - imag * sine, real * sine + imag * cosine)):
        high, low = split(value)
        high_ref[at, part * N : (part + 1) * N] = high
        low_ref[at, part * N : (part + 1) * N] = low


def head_kernel(miller_ref, rho_ref, shift_ref, support_ref, table_ref, left_ref, out_ref, high_ref, low_ref, ah_ref, al_ref):
    i = pl.program_id(0)
    r = lax.axis_index("refl")
    hkl = [miller_ref[c, r].astype(F32) for c in range(3)]
    now, before = lax.rem(i, 2), lax.rem(i + 1, 2)
    out_ref[:, 0] = left_split(left_ref[...], ah_ref[now], al_ref[now]).reshape(SLABS, XL, 2 * KC)
    high = high_ref[before]
    a = jnp.dot(jnp.concatenate([high, low_ref[before], high], 1), table_ref[...], preferred_element_type=F32)
    ah_ref[before], al_ref[before] = split(a)
    for row in range(0, N, HEAD_ROWS):
        object_rows(hkl, rho_ref, shift_ref, support_ref, high_ref.at[now], low_ref.at[now], row, HEAD_ROWS)


def x_kernel(in_ref, amp_ref, forward_ref, inverse_ref, *refs):
    out_ref, real_ref, imag_ref, sems = refs
    parts = ((real_ref, pl.ds(0, KC)), (imag_ref, pl.ds(KC, KC)))
    copies = [
        pltpu.make_async_copy(in_ref.at[:, lanes], part, sems.at[i]) for i, (part, lanes) in enumerate(parts)
    ]
    for copy in copies:
        copy.start()
    for copy in copies:
        copy.wait()

    def step(i, carry):
        at = pl.ds(i, N, stride=XL)
        spec = left_multiply(forward_ref[...], jnp.concatenate([real_ref[at, :], imag_ref[at, :]], 1))
        real, imag = spec[:, :KC], spec[:, KC:]
        ratio = amp_ref[at, :] * lax.rsqrt(jnp.maximum(real * real + imag * imag, 0.25))
        resid = jnp.concatenate([real - ratio * real, imag - ratio * imag], 1)
        back = left_multiply(inverse_ref[...], resid)
        real_ref[at, :] = back[:, :KC]
        imag_ref[at, :] = back[:, KC:]
        return carry

    lax.fori_loop(0, XL, step, 0)
    copies = [
        pltpu.make_async_copy(part, out_ref.at[:, lanes], sems.at[i]) for i, (part, lanes) in enumerate(parts)
    ]
    for copy in copies:
        copy.start()
    for copy in copies:
        copy.wait()


def partner(r, s, sign):
    return lax.rem(r // 2 + NREF // 2 + sign * (s // 2), NREF // 2) * 2 + lax.rem(r + s, 2)


def y_inverse_kernel(idx_ref, in_ref, table_ref, *refs):
    outs, t_ref = refs[:NREF], refs[NREF]
    r = idx_ref[0]

    def step(x, carry):
        t_ref[...] = left_multiply(table_ref[...], in_ref[:, x].reshape(N, 2 * KC))
        for s in range(NREF):
            start = pl.multiple_of(partner(r, s, 1) * 32, 32)
            outs[s][x] = t_ref[pl.ds(start, 32), :]
        return carry

    lax.fori_loop(0, XL, step, 0)


def gradient_kernel(shift_by, idx_ref, miller_ref, rho_ref, shift_ref, support_ref, *refs):
    ins, table_ref, sums = refs[:CH], refs[CH], refs[CH + 1 : -2]
    rho_out, shift_out = refs[-2:]
    g = partner(idx_ref[0], shift_by, -1)
    h, k, l = (miller_ref[c, g].astype(F32) for c in range(3))
    rows = pl.ds(pl.multiple_of(idx_ref[0] * 32, 32), 32)
    half = XL // 2
    backs = []
    for first in (0, half):
        packed = [ref[first : first + half].reshape(half * 32, 2 * KC) for ref in ins]
        high, low = split(jnp.concatenate(packed, 1))
        backs.append(
            jnp.dot(jnp.concatenate([high, low, high], 1), table_ref[...], preferred_element_type=F32)
        )
    for x in range(XL):
        back = backs[x // half][x % half * 32 : (x % half + 1) * 32]
        u = [shift_ref[c, x, rows, :].astype(F32) for c in range(3)]
        mask = support_ref[x, rows, :].astype(F32) * (1.0 / NREF)
        cosine, sine = cos_sin_turns(h * u[0] + k * u[1] + l * u[2])
        real, imag = back[:, :N], back[:, N:]
        p = mask * (cosine * real + sine * imag)
        q = mask * (cosine * imag - sine * real)
        twist = rho_ref[0, x, rows, :].astype(F32) * q - rho_ref[1, x, rows, :].astype(F32) * p
        for out, old, n, value in (
            (rho_out, 0, 0, p),
            (rho_out, 0, 1, q),
            (shift_out, 1, 0, h * twist),
            (shift_out, 1, 1, k * twist),
            (shift_out, 1, 2, l * twist),
        ):
            out[n, x] = sums[old][n, x] + value if sums else value


SMEM = pl.BlockSpec(memory_space=pltpu.SMEM)
VMEM = pl.BlockSpec(memory_space=pltpu.VMEM)
HBM = pl.BlockSpec(memory_space=pltpu.HBM)


def cost(flops, size):
    return pl.CostEstimate(flops=int(flops), bytes_accessed=int(size), transcendentals=0)


def f32(*shape):
    return jax.ShapeDtypeStruct(shape, F32)


def params(mib):
    return pltpu.CompilerParams(vmem_limit_bytes=mib * 1024 * 1024)


def hbm(*shape):
    return pltpu.HBM(shape, F32)


def in_hbm(value):
    return pltpu.with_memory_space_constraint(value, pltpu.HBM)


def after(value, *earlier):
    return lax.optimization_barrier((value, earlier))[0]


def head(c, millers, density, displacement, support):
    plane = lambda i: jnp.minimum(i, XL - 1)
    last = lambda i: jnp.maximum(i - 2, 0)
    return pl.pallas_call(
        head_kernel,
        grid=(XL + 2,),
        in_specs=[
            SMEM,
            pl.BlockSpec((2, 1, N, N), lambda i: (0, plane(i), 0, 0)),
            pl.BlockSpec((3, 1, N, N), lambda i: (0, plane(i), 0, 0)),
            pl.BlockSpec((1, N, N), lambda i: (plane(i), 0, 0)),
            pl.BlockSpec((6 * N, 2 * KC), lambda i: (0, c)),
            pl.BlockSpec((2 * N, 3 * N), lambda i: (0, 0)),
        ],
        out_specs=pl.BlockSpec((SLABS, 1, XL, 2 * KC), lambda i: (0, last(i), 0, 0)),
        out_shape=f32(SLABS, XL, XL, 2 * KC),
        scratch_shapes=[pltpu.VMEM((2, N, 2 * N), BF)] * 2 + [pltpu.VMEM((2, N, 2 * KC), BF)] * 2,
        compiler_params=params(60),
        cost_estimate=cost(6.4e9, 16e6),
        name=f"head_{c}",
    )(millers, density, displacement, support, jnp.asarray(right_forward()), jnp.asarray(left_table(False)))


def body(density, displacement, support, millers, amplitude):
    r = lax.axis_index("refl")
    idx = jnp.stack([r]).astype(jnp.int32)
    forward, inverse = jnp.asarray(left_table(False)), jnp.asarray(left_table(True))
    last_table = jnp.asarray(right_inverse())
    amp = amplitude.reshape(N * XL, N)
    millers = millers.T

    def x_both(c, part):
        return pl.pallas_call(
            x_kernel,
            grid=(1,),
            in_specs=[HBM, pl.BlockSpec((N * XL, KC), lambda i: (0, c)), VMEM, VMEM],
            out_specs=HBM,
            out_shape=hbm(N * XL, 2 * KC),
            scratch_shapes=[pltpu.VMEM((N * XL, KC), F32)] * 2 + [pltpu.SemaphoreType.DMA((2,))],
            compiler_params=params(24),
            cost_estimate=cost(6.4e9, 24e6),
            name=f"x_{c}",
        )(in_hbm(part.reshape(N * XL, 2 * KC)), amp, forward, inverse).reshape(SLABS, XL, XL, 2 * KC)

    def y_inverse(c, part):
        return pl.pallas_call(
            y_inverse_kernel,
            in_specs=[SMEM, VMEM, VMEM],
            out_specs=[VMEM] * NREF,
            out_shape=[f32(XL, 32, 2 * KC)] * NREF,
            scratch_shapes=[pltpu.VMEM((N, 2 * KC), F32)],
            compiler_params=params(24),
            cost_estimate=cost(3.2e9, 12e6),
            name=f"y_inverse_{c}",
        )(idx, part, inverse)

    def over_grid(part):
        return lax.all_to_all(part, "grid", 0, 0, tiled=True)

    def over_refl(parts):
        ring = lambda s: [(i, (i // 2 + s // 2) % (NREF // 2) * 2 + (i + s) % 2) for i in range(NREF)]
        moved = {s: lax.ppermute(parts[s], "refl", ring(s)) for s in R_ORDER}
        return [parts[0]] + [moved[s] for s in range(1, NREF)]

    def gradient(s, parts, sums):
        return tuple(
            pl.pallas_call(
                functools.partial(gradient_kernel, s),
                in_specs=[SMEM, SMEM] + [VMEM] * (3 + CH + 1 + len(sums)),
                out_specs=[VMEM] * 2,
                out_shape=[f32(2, XL, 32, N), f32(3, XL, 32, N)],
                compiler_params=params(16),
                cost_estimate=cost(0.8e9, 5e6),
                name=f"gradient_{s}",
            )(idx, millers, density, displacement, support, *parts, last_table, *sums)
        )

    f0 = over_grid(head(0, millers, density, displacement, support))
    f1 = over_grid(after(head(1, millers, density, displacement, support), f0))
    b0 = over_grid(after(x_both(0, f0), f1))
    b1 = over_grid(after(x_both(1, f1), b0))
    r0 = over_refl(y_inverse(0, in_hbm(b0)))
    parts = y_inverse(1, after(b1, *(r0[s] for s in R_ORDER[:5])))
    r1 = over_refl(after(parts, *r0))
    sums = ()
    for s in (0,) + R_ORDER:
        sums = gradient(s, (r0[s], r1[s]), sums)
    return sums


def solution(mesh):
    in_specs = (
        P(None, "grid", None, None),
        P(None, "grid", None, None),
        P("grid", None, None),
        P(),
        P("refl", None, "grid", None),
    )
    out_specs = (P(None, "grid", "refl", None), P(None, "grid", "refl", None))
    return jax.shard_map(body, mesh=mesh, in_specs=in_specs, out_specs=out_specs, check_vma=False)
```

```python
import functools
import math

import jax
import jax.numpy as jnp
import ml_dtypes
import numpy as np
from jax import lax
from jax.experimental import pallas as pl
from jax.experimental.pallas import tpu as pltpu
from jax.sharding import PartitionSpec as P

N = 256
CH = 2
KC = N // CH
SLABS = 32
XL = 8
NREF = 8
HEAD_ROWS = 32
R_ORDER = (5, 4, 1, 3, 7, 2, 6)
BF = jnp.bfloat16
F32 = jnp.float32


def split_np(table):
    high = table.astype(ml_dtypes.bfloat16)
    low = (table - high.astype(np.float64)).astype(ml_dtypes.bfloat16)
    return high, low


def dft_np():
    n = np.arange(N)
    angle = 2.0 * np.pi * (np.outer(n, n) % N) / N
    return np.cos(angle) / math.sqrt(N), -np.sin(angle) / math.sqrt(N)


def left_table(inverse):
    re, im = dft_np()
    high, low = split_np(np.concatenate([re, -im if inverse else im], 0))
    return np.concatenate([high, high, low], 1)


def packed_columns():
    chunk = np.arange(N) // KC
    inner = np.arange(N) % KC
    real = chunk * 2 * KC + inner
    return real, real + KC


def right_forward():
    re, im = dft_np()
    real, imag = packed_columns()
    table = np.zeros((2 * N, 2 * N))
    table[:N, real] = re
    table[:N, imag] = im
    table[N:, real] = -im
    table[N:, imag] = re
    high, low = split_np(table)
    return np.concatenate([high, high, low], 0)


def right_inverse():
    re, im = dft_np()
    real, imag = packed_columns()
    table = np.zeros((2 * N, 2 * N))
    table[real, :N] = re
    table[real, N:] = -im
    table[imag, :N] = im
    table[imag, N:] = re
    high, low = split_np(table)
    return np.concatenate([high, high, low], 0)


def sine_coefficients():
    b = 0.25 * np.cos((np.arange(400) + 0.5) / 400 * np.pi / 2)
    powers = np.stack([b ** (2 * k + 1) for k in range(6)], 1)
    return [float(v) for v in np.linalg.lstsq(powers, np.sin(2 * np.pi * b), rcond=None)[0]]


SINE = sine_coefficients()


def sine_turns(b):
    q = b * b
    acc = jnp.full_like(b, SINE[5])
    for k in range(4, -1, -1):
        acc = acc * q + SINE[k]
    return acc * b


def cos_sin_turns(t):
    t = t - jnp.round(t)
    cosine = sine_turns(0.25 - jnp.abs(t))
    u = t - 0.25
    u = u - jnp.round(u)
    return cosine, sine_turns(0.25 - jnp.abs(u))


def split(value):
    high = value.astype(BF)
    return high, (value - high.astype(F32)).astype(BF)


def left_multiply(table, packed):
    return left_split(table, *split(packed))


def left_split(table, high, low):
    both = jnp.dot(table, jnp.concatenate([high, low, high], 0), preferred_element_type=F32)
    real = both[:N, :KC] - both[N:, KC:]
    imag = both[:N, KC:] + both[N:, :KC]
    return jnp.concatenate([real, imag], 1)


def object_rows(hkl, rho_ref, shift_ref, support_ref, high_ref, low_ref, start, rows):
    at = pl.ds(start, rows)
    u = [shift_ref[c, 0, at, :].astype(F32) for c in range(3)]
    mask = support_ref[0, at, :].astype(F32)
    cosine, sine = cos_sin_turns(hkl[0] * u[0] + hkl[1] * u[1] + hkl[2] * u[2])
    real = mask * rho_ref[0, 0, at, :].astype(F32)
    imag = mask * rho_ref[1, 0, at, :].astype(F32)
    for part, value in enumerate((real * cosine - imag * sine, real * sine + imag * cosine)):
        high, low = split(value)
        high_ref[at, part * N : (part + 1) * N] = high
        low_ref[at, part * N : (part + 1) * N] = low


def head_kernel(miller_ref, rho_ref, shift_ref, support_ref, table_ref, left_ref, out_ref, high_ref, low_ref, ah_ref, al_ref):
    i = pl.program_id(0)
    r = lax.axis_index("refl")
    hkl = [miller_ref[c, r].astype(F32) for c in range(3)]
    now, before = lax.rem(i, 2), lax.rem(i + 1, 2)
    out_ref[:, 0] = left_split(left_ref[...], ah_ref[now], al_ref[now]).reshape(SLABS, XL, 2 * KC)
    high = high_ref[before]
    a = jnp.dot(jnp.concatenate([high, low_ref[before], high], 1), table_ref[...], preferred_element_type=F32)
    ah_ref[before], al_ref[before] = split(a)
    for row in range(0, N, HEAD_ROWS):
        object_rows(hkl, rho_ref, shift_ref, support_ref, high_ref.at[now], low_ref.at[now], row, HEAD_ROWS)


def x_kernel(in_ref, amp_ref, forward_ref, inverse_ref, *refs):
    out_ref, real_ref, imag_ref, sems = refs
    parts = ((real_ref, pl.ds(0, KC)), (imag_ref, pl.ds(KC, KC)))
    copies = [
        pltpu.make_async_copy(in_ref.at[:, lanes], part, sems.at[i]) for i, (part, lanes) in enumerate(parts)
    ]
    for copy in copies:
        copy.start()
    for copy in copies:
        copy.wait()

    def step(i, carry):
        at = pl.ds(i, N, stride=XL)
        spec = left_multiply(forward_ref[...], jnp.concatenate([real_ref[at, :], imag_ref[at, :]], 1))
        real, imag = spec[:, :KC], spec[:, KC:]
        ratio = amp_ref[at, :] * lax.rsqrt(jnp.maximum(real * real + imag * imag, 0.25))
        resid = jnp.concatenate([real - ratio * real, imag - ratio * imag], 1)
        back = left_multiply(inverse_ref[...], resid)
        real_ref[at, :] = back[:, :KC]
        imag_ref[at, :] = back[:, KC:]
        return carry

    lax.fori_loop(0, XL, step, 0)
    copies = [
        pltpu.make_async_copy(part, out_ref.at[:, lanes], sems.at[i]) for i, (part, lanes) in enumerate(parts)
    ]
    for copy in copies:
        copy.start()
    for copy in copies:
        copy.wait()


def partner(r, s, sign):
    return lax.rem(r // 2 + NREF // 2 + sign * (s // 2), NREF // 2) * 2 + lax.rem(r + s, 2)


def y_inverse_kernel(idx_ref, in_ref, table_ref, *refs):
    outs, t_ref = refs[:NREF], refs[NREF]
    r = idx_ref[0]

    def step(x, carry):
        t_ref[...] = left_multiply(table_ref[...], in_ref[:, x].reshape(N, 2 * KC))
        for s in range(NREF):
            start = pl.multiple_of(partner(r, s, 1) * 32, 32)
            outs[s][x] = t_ref[pl.ds(start, 32), :]
        return carry

    lax.fori_loop(0, XL, step, 0)


def gradient_kernel(shift_by, idx_ref, miller_ref, rho_ref, shift_ref, support_ref, *refs):
    ins, table_ref, sums = refs[:CH], refs[CH], refs[CH + 1 : -2]
    rho_out, shift_out = refs[-2:]
    g = partner(idx_ref[0], shift_by, -1)
    h, k, l = (miller_ref[c, g].astype(F32) for c in range(3))
    rows = pl.ds(pl.multiple_of(idx_ref[0] * 32, 32), 32)
    half = XL // 2
    backs = []
    for first in (0, half):
        packed = [ref[first : first + half].reshape(half * 32, 2 * KC) for ref in ins]
        high, low = split(jnp.concatenate(packed, 1))
        backs.append(
            jnp.dot(jnp.concatenate([high, low, high], 1), table_ref[...], preferred_element_type=F32)
        )
    for x in range(XL):
        back = backs[x // half][x % half * 32 : (x % half + 1) * 32]
        u = [shift_ref[c, x, rows, :].astype(F32) for c in range(3)]
        mask = support_ref[x, rows, :].astype(F32) * (1.0 / NREF)
        cosine, sine = cos_sin_turns(h * u[0] + k * u[1] + l * u[2])
        real, imag = back[:, :N], back[:, N:]
        p = mask * (cosine * real + sine * imag)
        q = mask * (cosine * imag - sine * real)
        twist = rho_ref[0, x, rows, :].astype(F32) * q - rho_ref[1, x, rows, :].astype(F32) * p
        for out, old, n, value in (
            (rho_out, 0, 0, p),
            (rho_out, 0, 1, q),
            (shift_out, 1, 0, h * twist),
            (shift_out, 1, 1, k * twist),
            (shift_out, 1, 2, l * twist),
        ):
            out[n, x] = sums[old][n, x] + value if sums else value


def early_kernel(shift_by, idx_ref, miller_ref, shift_ref, support_ref, in_ref, table_ref, back_ref, phase_ref):
    g = partner(idx_ref[0], shift_by, -1)
    h, k, l = (miller_ref[c, g].astype(F32) for c in range(3))
    rows = pl.ds(pl.multiple_of(idx_ref[0] * 32, 32), 32)
    high, low = split(in_ref[...].reshape(N, 2 * KC))
    back_ref[...] = jnp.dot(
        jnp.concatenate([high, low, high], 1), table_ref[...], preferred_element_type=F32
    )
    for x in range(XL):
        u = [shift_ref[c, x, rows, :].astype(F32) for c in range(3)]
        mask = support_ref[x, rows, :].astype(F32) * (1.0 / NREF)
        cosine, sine = cos_sin_turns(h * u[0] + k * u[1] + l * u[2])
        phase_ref[0, x] = mask * cosine
        phase_ref[1, x] = mask * sine


def late_kernel(shift_by, idx_ref, miller_ref, rho_ref, in_ref, back_ref, phase_ref, table_ref, *refs):
    sums, (rho_out, shift_out) = refs[:2], refs[2:]
    g = partner(idx_ref[0], shift_by, -1)
    hkl = [miller_ref[c, g].astype(F32) for c in range(3)]
    rows = pl.ds(pl.multiple_of(idx_ref[0] * 32, 32), 32)
    high, low = split(in_ref[...].reshape(N, 2 * KC))
    rest = jnp.dot(jnp.concatenate([high, low, high], 1), table_ref[...], preferred_element_type=F32)
    for x in range(XL):
        at = slice(x * 32, (x + 1) * 32)
        back = back_ref[at, :] + rest[at]
        real, imag = back[:, :N], back[:, N:]
        cosine, sine = phase_ref[0, x], phase_ref[1, x]
        p = cosine * real + sine * imag
        q = cosine * imag - sine * real
        twist = rho_ref[0, x, rows, :].astype(F32) * q - rho_ref[1, x, rows, :].astype(F32) * p
        rho_out[0, x] = sums[0][0, x] + p
        rho_out[1, x] = sums[0][1, x] + q
        for c in range(3):
            shift_out[c, x] = sums[1][c, x] + hkl[c] * twist


SMEM = pl.BlockSpec(memory_space=pltpu.SMEM)
VMEM = pl.BlockSpec(memory_space=pltpu.VMEM)
HBM = pl.BlockSpec(memory_space=pltpu.HBM)


def cost(flops, size):
    return pl.CostEstimate(flops=int(flops), bytes_accessed=int(size), transcendentals=0)


def f32(*shape):
    return jax.ShapeDtypeStruct(shape, F32)


def params(mib):
    return pltpu.CompilerParams(vmem_limit_bytes=mib * 1024 * 1024)


def hbm(*shape):
    return pltpu.HBM(shape, F32)


def in_hbm(value):
    return pltpu.with_memory_space_constraint(value, pltpu.HBM)


def after(value, *earlier):
    return lax.optimization_barrier((value, earlier))[0]


def head(c, millers, density, displacement, support):
    plane = lambda i: jnp.minimum(i, XL - 1)
    last = lambda i: jnp.maximum(i - 2, 0)
    return pl.pallas_call(
        head_kernel,
        grid=(XL + 2,),
        in_specs=[
            SMEM,
            pl.BlockSpec((2, 1, N, N), lambda i: (0, plane(i), 0, 0)),
            pl.BlockSpec((3, 1, N, N), lambda i: (0, plane(i), 0, 0)),
            pl.BlockSpec((1, N, N), lambda i: (plane(i), 0, 0)),
            pl.BlockSpec((6 * N, 2 * KC), lambda i: (0, c)),
            pl.BlockSpec((2 * N, 3 * N), lambda i: (0, 0)),
        ],
        out_specs=pl.BlockSpec((SLABS, 1, XL, 2 * KC), lambda i: (0, last(i), 0, 0)),
        out_shape=f32(SLABS, XL, XL, 2 * KC),
        scratch_shapes=[pltpu.VMEM((2, N, 2 * N), BF)] * 2 + [pltpu.VMEM((2, N, 2 * KC), BF)] * 2,
        compiler_params=params(60),
        cost_estimate=cost(6.4e9, 16e6),
        name=f"head_{c}",
    )(millers, density, displacement, support, jnp.asarray(right_forward()), jnp.asarray(left_table(False)))


def body(density, displacement, support, millers, amplitude):
    r = lax.axis_index("refl")
    idx = jnp.stack([r]).astype(jnp.int32)
    forward, inverse = jnp.asarray(left_table(False)), jnp.asarray(left_table(True))
    last_table = jnp.asarray(right_inverse())
    tables = [
        jnp.asarray(right_inverse().reshape(3, CH, 2 * KC, 2 * N)[:, c].reshape(6 * KC, 2 * N)) for c in range(CH)
    ]
    amp = amplitude.reshape(N * XL, N)
    millers = millers.T

    def x_both(c, part):
        return pl.pallas_call(
            x_kernel,
            grid=(1,),
            in_specs=[HBM, pl.BlockSpec((N * XL, KC), lambda i: (0, c)), VMEM, VMEM],
            out_specs=HBM,
            out_shape=hbm(N * XL, 2 * KC),
            scratch_shapes=[pltpu.VMEM((N * XL, KC), F32)] * 2 + [pltpu.SemaphoreType.DMA((2,))],
            compiler_params=params(24),
            cost_estimate=cost(6.4e9, 24e6),
            name=f"x_{c}",
        )(in_hbm(part.reshape(N * XL, 2 * KC)), amp, forward, inverse).reshape(SLABS, XL, XL, 2 * KC)

    def y_inverse(c, part):
        return pl.pallas_call(
            y_inverse_kernel,
            in_specs=[SMEM, VMEM, VMEM],
            out_specs=[VMEM] * NREF,
            out_shape=[f32(XL, 32, 2 * KC)] * NREF,
            scratch_shapes=[pltpu.VMEM((N, 2 * KC), F32)],
            compiler_params=params(24),
            cost_estimate=cost(3.2e9, 12e6),
            name=f"y_inverse_{c}",
        )(idx, part, inverse)

    def over_grid(part):
        return lax.all_to_all(part, "grid", 0, 0, tiled=True)

    def over_refl(parts):
        ring = lambda s: [(i, (i // 2 + s // 2) % (NREF // 2) * 2 + (i + s) % 2) for i in range(NREF)]
        moved = {s: lax.ppermute(parts[s], "refl", ring(s)) for s in R_ORDER}
        return [parts[0]] + [moved[s] for s in range(1, NREF)]

    def gradient(s, parts, sums):
        return tuple(
            pl.pallas_call(
                functools.partial(gradient_kernel, s),
                in_specs=[SMEM, SMEM] + [VMEM] * (3 + CH + 1 + len(sums)),
                out_specs=[VMEM] * 2,
                out_shape=[f32(2, XL, 32, N), f32(3, XL, 32, N)],
                compiler_params=params(16),
                cost_estimate=cost(0.8e9, 5e6),
                name=f"gradient_{s}",
            )(idx, millers, density, displacement, support, *parts, last_table, *sums)
        )

    def early(s, part):
        return pl.pallas_call(
            functools.partial(early_kernel, s),
            in_specs=[SMEM, SMEM] + [VMEM] * 4,
            out_specs=[VMEM] * 2,
            out_shape=[f32(N, 2 * N), f32(2, XL, 32, N)],
            compiler_params=params(16),
            cost_estimate=cost(0.8e9, 5e6),
            name=f"early_{s}",
        )(idx, millers, displacement, support, part, tables[0])

    def late(s, part, known, sums):
        return tuple(
            pl.pallas_call(
                functools.partial(late_kernel, s),
                in_specs=[SMEM, SMEM] + [VMEM] * 7,
                out_specs=[VMEM] * 2,
                out_shape=[f32(2, XL, 32, N), f32(3, XL, 32, N)],
                compiler_params=params(16),
                cost_estimate=cost(0.4e9, 5e6),
                name=f"late_{s}",
            )(idx, millers, density, part, *known, tables[1], *sums)
        )

    f0 = over_grid(head(0, millers, density, displacement, support))
    f1 = over_grid(after(head(1, millers, density, displacement, support), f0))
    b0 = over_grid(after(x_both(0, f0), f1))
    b1 = over_grid(after(x_both(1, f1), b0))
    r0 = over_refl(y_inverse(0, in_hbm(b0)))
    parts = y_inverse(1, after(b1, *(r0[s] for s in R_ORDER[:5])))
    r1 = over_refl(after(parts, *r0))
    sums = ()
    for s in (0,) + R_ORDER[:2]:
        sums = gradient(s, (r0[s], r1[s]), sums)
    known = {s: early(s, after(r0[s], r1[R_ORDER[0]])) for s in R_ORDER[2:]}
    sums = after(sums, known)
    for s in R_ORDER[2:]:
        sums = late(s, r1[s], known[s], sums)
    return sums


def solution(mesh):
    in_specs = (
        P(None, "grid", None, None),
        P(None, "grid", None, None),
        P("grid", None, None),
        P(),
        P("refl", None, "grid", None),
    )
    out_specs = (P(None, "grid", "refl", None), P(None, "grid", "refl", None))
    return jax.shard_map(body, mesh=mesh, in_specs=in_specs, out_specs=out_specs, check_vma=False)
```

```python
import functools
import math

import jax
import jax.numpy as jnp
import ml_dtypes
import numpy as np
from jax import lax
from jax.experimental import pallas as pl
from jax.experimental.pallas import tpu as pltpu
from jax.sharding import PartitionSpec as P

N = 256
CH = 2
KC = N // CH
SLABS = 32
XL = 8
NREF = 8
HEAD_ROWS = 32
R_ORDER = (5, 4, 1, 3, 7, 2, 6)
BF = jnp.bfloat16
F32 = jnp.float32


def split_np(table):
    high = table.astype(ml_dtypes.bfloat16)
    low = (table - high.astype(np.float64)).astype(ml_dtypes.bfloat16)
    return high, low


def dft_np():
    n = np.arange(N)
    angle = 2.0 * np.pi * (np.outer(n, n) % N) / N
    return np.cos(angle) / math.sqrt(N), -np.sin(angle) / math.sqrt(N)


def left_table(inverse):
    re, im = dft_np()
    high, low = split_np(np.concatenate([re, -im if inverse else im], 0))
    return np.concatenate([high, high, low], 1)


def packed_columns():
    chunk = np.arange(N) // KC
    inner = np.arange(N) % KC
    real = chunk * 2 * KC + inner
    return real, real + KC


def right_forward():
    re, im = dft_np()
    real, imag = packed_columns()
    table = np.zeros((2 * N, 2 * N))
    table[:N, real] = re
    table[:N, imag] = im
    table[N:, real] = -im
    table[N:, imag] = re
    high, low = split_np(table)
    return np.concatenate([high, high, low], 0)


def right_inverse():
    re, im = dft_np()
    real, imag = packed_columns()
    table = np.zeros((2 * N, 2 * N))
    table[real, :N] = re
    table[real, N:] = -im
    table[imag, :N] = im
    table[imag, N:] = re
    high, low = split_np(table)
    return np.concatenate([high, high, low], 0)


def sine_coefficients():
    b = 0.25 * np.cos((np.arange(400) + 0.5) / 400 * np.pi / 2)
    powers = np.stack([b ** (2 * k + 1) for k in range(6)], 1)
    return [float(v) for v in np.linalg.lstsq(powers, np.sin(2 * np.pi * b), rcond=None)[0]]


SINE = sine_coefficients()


def sine_turns(b):
    q = b * b
    acc = jnp.full_like(b, SINE[5])
    for k in range(4, -1, -1):
        acc = acc * q + SINE[k]
    return acc * b


def cos_sin_turns(t):
    t = t - jnp.round(t)
    cosine = sine_turns(0.25 - jnp.abs(t))
    u = t - 0.25
    u = u - jnp.round(u)
    return cosine, sine_turns(0.25 - jnp.abs(u))


def split(value):
    high = value.astype(BF)
    return high, (value - high.astype(F32)).astype(BF)


def left_multiply(table, packed):
    return left_split(table, *split(packed))


def left_split(table, high, low):
    both = jnp.dot(table, jnp.concatenate([high, low, high], 0), preferred_element_type=F32)
    real = both[:N, :KC] - both[N:, KC:]
    imag = both[:N, KC:] + both[N:, :KC]
    return jnp.concatenate([real, imag], 1)


def object_rows(hkl, rho_ref, shift_ref, support_ref, high_ref, low_ref, start, rows):
    at = pl.ds(start, rows)
    u = [shift_ref[c, 0, at, :].astype(F32) for c in range(3)]
    mask = support_ref[0, at, :].astype(F32)
    cosine, sine = cos_sin_turns(hkl[0] * u[0] + hkl[1] * u[1] + hkl[2] * u[2])
    real = mask * rho_ref[0, 0, at, :].astype(F32)
    imag = mask * rho_ref[1, 0, at, :].astype(F32)
    for part, value in enumerate((real * cosine - imag * sine, real * sine + imag * cosine)):
        high, low = split(value)
        high_ref[at, part * N : (part + 1) * N] = high
        low_ref[at, part * N : (part + 1) * N] = low


def head_kernel(miller_ref, rho_ref, shift_ref, support_ref, table_ref, left_ref, out_ref, high_ref, low_ref, ah_ref, al_ref):
    i = pl.program_id(0)
    r = lax.axis_index("refl")
    hkl = [miller_ref[c, r].astype(F32) for c in range(3)]
    now, before = lax.rem(i, 2), lax.rem(i + 1, 2)
    out_ref[:, 0] = left_split(left_ref[...], ah_ref[now], al_ref[now]).reshape(SLABS, XL, 2 * KC)
    high = high_ref[before]
    a = jnp.dot(jnp.concatenate([high, low_ref[before], high], 1), table_ref[...], preferred_element_type=F32)
    ah_ref[before], al_ref[before] = split(a)
    for row in range(0, N, HEAD_ROWS):
        object_rows(hkl, rho_ref, shift_ref, support_ref, high_ref.at[now], low_ref.at[now], row, HEAD_ROWS)


def x_kernel(in_ref, amp_ref, forward_ref, inverse_ref, *refs):
    out_ref, real_ref, imag_ref, sems = refs
    parts = ((real_ref, pl.ds(0, KC)), (imag_ref, pl.ds(KC, KC)))
    copies = [
        pltpu.make_async_copy(in_ref.at[:, lanes], part, sems.at[i]) for i, (part, lanes) in enumerate(parts)
    ]
    for copy in copies:
        copy.start()
    for copy in copies:
        copy.wait()

    def step(i, carry):
        at = pl.ds(i, N, stride=XL)
        spec = left_multiply(forward_ref[...], jnp.concatenate([real_ref[at, :], imag_ref[at, :]], 1))
        real, imag = spec[:, :KC], spec[:, KC:]
        ratio = amp_ref[at, :] * lax.rsqrt(jnp.maximum(real * real + imag * imag, 0.25))
        resid = jnp.concatenate([real - ratio * real, imag - ratio * imag], 1)
        back = left_multiply(inverse_ref[...], resid)
        real_ref[at, :] = back[:, :KC]
        imag_ref[at, :] = back[:, KC:]
        return carry

    lax.fori_loop(0, XL, step, 0)
    copies = [
        pltpu.make_async_copy(part, out_ref.at[:, lanes], sems.at[i]) for i, (part, lanes) in enumerate(parts)
    ]
    for copy in copies:
        copy.start()
    for copy in copies:
        copy.wait()


def partner(r, s, sign):
    return lax.rem(r // 2 + NREF // 2 + sign * (s // 2), NREF // 2) * 2 + lax.rem(r + s, 2)


def y_inverse_kernel(idx_ref, in_ref, table_ref, *refs):
    outs, t_ref = refs[:NREF], refs[NREF]
    r = idx_ref[0]

    def step(x, carry):
        t_ref[...] = left_multiply(table_ref[...], in_ref[:, x].reshape(N, 2 * KC))
        for s in range(NREF):
            start = pl.multiple_of(partner(r, s, 1) * 32, 32)
            outs[s][x] = t_ref[pl.ds(start, 32), :]
        return carry

    lax.fori_loop(0, XL, step, 0)


def gradient_kernel(shift_by, idx_ref, miller_ref, rho_ref, shift_ref, support_ref, *refs):
    ins, table_ref, sums = refs[:CH], refs[CH], refs[CH + 1 : -2]
    rho_out, shift_out = refs[-2:]
    g = partner(idx_ref[0], shift_by, -1)
    h, k, l = (miller_ref[c, g].astype(F32) for c in range(3))
    rows = pl.ds(pl.multiple_of(idx_ref[0] * 32, 32), 32)
    half = XL // 2
    backs = []
    for first in (0, half):
        packed = [ref[first : first + half].reshape(half * 32, 2 * KC) for ref in ins]
        high, low = split(jnp.concatenate(packed, 1))
        backs.append(
            jnp.dot(jnp.concatenate([high, low, high], 1), table_ref[...], preferred_element_type=F32)
        )
    for x in range(XL):
        back = backs[x // half][x % half * 32 : (x % half + 1) * 32]
        u = [shift_ref[c, x, rows, :].astype(F32) for c in range(3)]
        mask = support_ref[x, rows, :].astype(F32) * (1.0 / NREF)
        cosine, sine = cos_sin_turns(h * u[0] + k * u[1] + l * u[2])
        real, imag = back[:, :N], back[:, N:]
        p = mask * (cosine * real + sine * imag)
        q = mask * (cosine * imag - sine * real)
        twist = rho_ref[0, x, rows, :].astype(F32) * q - rho_ref[1, x, rows, :].astype(F32) * p
        for out, old, n, value in (
            (rho_out, 0, 0, p),
            (rho_out, 0, 1, q),
            (shift_out, 1, 0, h * twist),
            (shift_out, 1, 1, k * twist),
            (shift_out, 1, 2, l * twist),
        ):
            out[n, x] = sums[old][n, x] + value if sums else value


def early_kernel(shift_by, idx_ref, miller_ref, shift_ref, support_ref, in_ref, table_ref, back_ref, phase_ref):
    g = partner(idx_ref[0], shift_by, -1)
    h, k, l = (miller_ref[c, g].astype(F32) for c in range(3))
    rows = pl.ds(pl.multiple_of(idx_ref[0] * 32, 32), 32)
    high, low = split(in_ref[...].reshape(N, 2 * KC))
    back_ref[...] = jnp.dot(
        jnp.concatenate([high, low, high], 1), table_ref[...], preferred_element_type=F32
    )
    for x in range(XL):
        u = [shift_ref[c, x, rows, :].astype(F32) for c in range(3)]
        mask = support_ref[x, rows, :].astype(F32) * (1.0 / NREF)
        cosine, sine = cos_sin_turns(h * u[0] + k * u[1] + l * u[2])
        phase_ref[0, x] = mask * cosine
        phase_ref[1, x] = mask * sine


def late_kernel(shift_by, idx_ref, miller_ref, rho_ref, in_ref, back_ref, phase_ref, table_ref, *refs):
    sums, (rho_out, shift_out) = refs[:2], refs[2:]
    g = partner(idx_ref[0], shift_by, -1)
    hkl = [miller_ref[c, g].astype(F32) for c in range(3)]
    rows = pl.ds(pl.multiple_of(idx_ref[0] * 32, 32), 32)
    high, low = split(in_ref[...].reshape(N, 2 * KC))
    rest = jnp.dot(jnp.concatenate([high, low, high], 1), table_ref[...], preferred_element_type=F32)
    for x in range(XL):
        at = slice(x * 32, (x + 1) * 32)
        back = back_ref[at, :] + rest[at]
        real, imag = back[:, :N], back[:, N:]
        cosine, sine = phase_ref[0, x], phase_ref[1, x]
        p = cosine * real + sine * imag
        q = cosine * imag - sine * real
        twist = rho_ref[0, x, rows, :].astype(F32) * q - rho_ref[1, x, rows, :].astype(F32) * p
        rho_out[0, x] = sums[0][0, x] + p
        rho_out[1, x] = sums[0][1, x] + q
        for c in range(3):
            shift_out[c, x] = sums[1][c, x] + hkl[c] * twist


SMEM = pl.BlockSpec(memory_space=pltpu.SMEM)
VMEM = pl.BlockSpec(memory_space=pltpu.VMEM)
HBM = pl.BlockSpec(memory_space=pltpu.HBM)


def cost(flops, size):
    return pl.CostEstimate(flops=int(flops), bytes_accessed=int(size), transcendentals=0)


def f32(*shape):
    return jax.ShapeDtypeStruct(shape, F32)


def params(mib):
    return pltpu.CompilerParams(vmem_limit_bytes=mib * 1024 * 1024)


def hbm(*shape):
    return pltpu.HBM(shape, F32)


def in_hbm(value):
    return pltpu.with_memory_space_constraint(value, pltpu.HBM)


def after(value, *earlier):
    return lax.optimization_barrier((value, earlier))[0]


def head(c, millers, density, displacement, support):
    plane = lambda i: jnp.minimum(i, XL - 1)
    last = lambda i: jnp.maximum(i - 2, 0)
    return pl.pallas_call(
        head_kernel,
        grid=(XL + 2,),
        in_specs=[
            SMEM,
            pl.BlockSpec((2, 1, N, N), lambda i: (0, plane(i), 0, 0)),
            pl.BlockSpec((3, 1, N, N), lambda i: (0, plane(i), 0, 0)),
            pl.BlockSpec((1, N, N), lambda i: (plane(i), 0, 0)),
            pl.BlockSpec((6 * N, 2 * KC), lambda i: (0, c)),
            pl.BlockSpec((2 * N, 3 * N), lambda i: (0, 0)),
        ],
        out_specs=pl.BlockSpec((SLABS, 1, XL, 2 * KC), lambda i: (0, last(i), 0, 0)),
        out_shape=f32(SLABS, XL, XL, 2 * KC),
        scratch_shapes=[pltpu.VMEM((2, N, 2 * N), BF)] * 2 + [pltpu.VMEM((2, N, 2 * KC), BF)] * 2,
        compiler_params=params(60),
        cost_estimate=cost(6.4e9, 16e6),
        name=f"head_{c}",
    )(millers, density, displacement, support, jnp.asarray(right_forward()), jnp.asarray(left_table(False)))


def body(density, displacement, support, millers, amplitude):
    r = lax.axis_index("refl")
    idx = jnp.stack([r]).astype(jnp.int32)
    forward, inverse = jnp.asarray(left_table(False)), jnp.asarray(left_table(True))
    last_table = jnp.asarray(right_inverse())
    tables = [
        jnp.asarray(right_inverse().reshape(3, CH, 2 * KC, 2 * N)[:, c].reshape(6 * KC, 2 * N)) for c in range(CH)
    ]
    amp = amplitude.reshape(N * XL, N)
    millers = millers.T

    def x_both(c, part):
        return pl.pallas_call(
            x_kernel,
            grid=(1,),
            in_specs=[HBM, pl.BlockSpec((N * XL, KC), lambda i: (0, c)), VMEM, VMEM],
            out_specs=HBM,
            out_shape=hbm(N * XL, 2 * KC),
            scratch_shapes=[pltpu.VMEM((N * XL, KC), F32)] * 2 + [pltpu.SemaphoreType.DMA((2,))],
            compiler_params=params(24),
            cost_estimate=cost(6.4e9, 24e6),
            name=f"x_{c}",
        )(in_hbm(part.reshape(N * XL, 2 * KC)), amp, forward, inverse).reshape(SLABS, XL, XL, 2 * KC)

    def y_inverse(c, part):
        return pl.pallas_call(
            y_inverse_kernel,
            in_specs=[SMEM, VMEM, VMEM],
            out_specs=[VMEM] * NREF,
            out_shape=[f32(XL, 32, 2 * KC)] * NREF,
            scratch_shapes=[pltpu.VMEM((N, 2 * KC), F32)],
            compiler_params=params(24),
            cost_estimate=cost(3.2e9, 12e6),
            name=f"y_inverse_{c}",
        )(idx, part, inverse)

    def over_grid(part):
        return lax.all_to_all(part, "grid", 0, 0, tiled=True)

    def over_refl(parts):
        ring = lambda s: [(i, (i // 2 + s // 2) % (NREF // 2) * 2 + (i + s) % 2) for i in range(NREF)]
        moved = {}
        for s in R_ORDER:
            part = after(parts[s], moved[R_ORDER[0]]) if s in R_ORDER[5:] else parts[s]
            moved[s] = lax.ppermute(part, "refl", ring(s))
        return [parts[0]] + [moved[s] for s in range(1, NREF)]

    def gradient(s, parts, sums):
        return tuple(
            pl.pallas_call(
                functools.partial(gradient_kernel, s),
                in_specs=[SMEM, SMEM] + [VMEM] * (3 + CH + 1 + len(sums)),
                out_specs=[VMEM] * 2,
                out_shape=[f32(2, XL, 32, N), f32(3, XL, 32, N)],
                compiler_params=params(16),
                cost_estimate=cost(0.8e9, 5e6),
                name=f"gradient_{s}",
            )(idx, millers, density, displacement, support, *parts, last_table, *sums)
        )

    def early(s, part):
        return pl.pallas_call(
            functools.partial(early_kernel, s),
            in_specs=[SMEM, SMEM] + [VMEM] * 4,
            out_specs=[VMEM] * 2,
            out_shape=[f32(N, 2 * N), f32(2, XL, 32, N)],
            compiler_params=params(16),
            cost_estimate=cost(0.8e9, 5e6),
            name=f"early_{s}",
        )(idx, millers, displacement, support, part, tables[0])

    def late(s, part, known, sums):
        return tuple(
            pl.pallas_call(
                functools.partial(late_kernel, s),
                in_specs=[SMEM, SMEM] + [VMEM] * 7,
                out_specs=[VMEM] * 2,
                out_shape=[f32(2, XL, 32, N), f32(3, XL, 32, N)],
                compiler_params=params(16),
                cost_estimate=cost(0.4e9, 5e6),
                name=f"late_{s}",
            )(idx, millers, density, part, *known, tables[1], *sums)
        )

    f0 = over_grid(head(0, millers, density, displacement, support))
    f1 = over_grid(after(head(1, millers, density, displacement, support), f0))
    b0 = over_grid(after(x_both(0, f0), f1))
    b1 = over_grid(after(x_both(1, f1), b0))
    r0 = over_refl(y_inverse(0, in_hbm(b0)))
    parts = y_inverse(1, after(b1, *(r0[s] for s in R_ORDER[:5])))
    r1 = over_refl(after(parts, *r0))
    sums = ()
    for s in (0,) + R_ORDER[:2]:
        sums = gradient(s, (r0[s], r1[s]), sums)
    known = {s: early(s, after(r0[s], r1[R_ORDER[0]])) for s in R_ORDER[2:]}
    sums = after(sums, known)
    for s in (2, 1, 3, 7, 6):
        sums = late(s, r1[s], known[s], sums)
    return sums


def solution(mesh):
    in_specs = (
        P(None, "grid", None, None),
        P(None, "grid", None, None),
        P("grid", None, None),
        P(),
        P("refl", None, "grid", None),
    )
    out_specs = (P(None, "grid", "refl", None), P(None, "grid", "refl", None))
    return jax.shard_map(body, mesh=mesh, in_specs=in_specs, out_specs=out_specs, check_vma=False)
```
